256 devices in a mesh: child: 2 (over core), row: 8 (over z), col: 16 (over x, y).
Axes of the slice: x: 4, y: 4, z: 8, core: 2. Of those that a mesh axis runs over, the one named last changes fastest.
Arguments:
- parent_slab: float32 [3072, 61440], P('col', ('child', 'row')), may hold values from -6 to 6
- panel: float32 [2, 16384, 1024], P('child', 'row'), may hold values from -0.0625 to 0.0625
- slab_panel: float32 [2, 3072, 1024], P('child', 'col'), may hold values from -0.15625 to 0.15625
- diag_inverse: float32 [2, 1024, 1024], P('child', 'col', 'row'), may hold values from -6 to 6
- tile_rows: int32 [2, 128, 128], replicated, may hold values from -1 to 3839, as said below
- tile_owner: int32 [2, 128, 1], replicated, may hold values from 0 to 15; in each aligned block of 16 rows (0 to 15, 16 to 31, ..., all dimensions but the last counted through in order) at most 2 rows name the same one
Outputs:
- slab_inverse: float32 [2, 3072, 1024], P('child', 'col', 'row')
- diag_block: float32 [2, 1024, 1024], P('child', 'col', 'row')
The draws below stay inside these ranges and needn't reach their ends.
Inputs may be any that keep to these rules, and one draw needn't show every extreme that they name: `tile_rows`: A tile's offsets lie in the column block of its owner; -1 marks padding and fills only the end of a tile. `tile_owner`: among the 16 tiles of one device (aligned blocks of one child), no owner holds more than 2.
All inputs are finite; a program needn't handle non-finite values.
Results may differ from the reference program's by a relative error of at most 0.0001.
Values sent between devices are 32-bit elements; how exact they have to be, the bound alone decides.
No kernel may reach another device: no remote copies, remote signals or barrier semaphores. Data moves between devices by JAX's collectives and lax.ppermute only.
A program may use at most 128 MiB of HBM per device.

```python
import math
import jax
import jax.numpy as jnp
import numpy as np
from jax import lax

B = 1024
PAR = 61440
TILE = 128
CAP = 2
TILE_DEV = 16
SLAB = 3072
NT = 128
NU = 16384
N_CHILD = 2
N_ROW = 8


def draw_tile_rows(key, part):
    key = jax.random.fold_in(key, 11)
    first_key, second_key = jax.random.split(key)
    block_cols = PAR // (N_CHILD * N_ROW)
    offsets = jax.random.randint(first_key, (N_CHILD, NT, TILE), 0, block_cols)
    padding = jax.random.randint(second_key, (N_CHILD, NT, 1), 1, TILE * 3 // 4 + 1)
    positions = lax.broadcasted_iota(jnp.int32, (N_CHILD, NT, TILE), 2)
    offsets = jnp.where(positions >= TILE - padding, -1, offsets)
    offsets = offsets.at[0, 0, 0].set(block_cols - 1)
    return offsets.astype(jnp.int32)


def spiked(entries, key, source, target, shards_of, factor):
    def block_of(position):
        return (jnp.arange(entries.shape[position]) // (entries.shape[position] // shards_of)).reshape((-1,) + (1,) * (entries.ndim - 1 - position))

    near = jax.random.permutation(key, shards_of)[block_of(target)]
    second = (block_of(target) + shards_of // 2) % shards_of
    return jnp.where((block_of(source) == near) | (block_of(source) == second), factor * entries, entries)


def block_scale(key, shape, shards, low, top_value):
    loudness, own = 1.0, jax.random.fold_in(key, 6)
    for dim, blocks in shards:
        steps = jnp.exp(jax.random.uniform(jax.random.fold_in(own, dim), (blocks,), jnp.float32, low / len(shards), top_value / len(shards)))
        loudness = loudness * jnp.repeat(steps, shape[dim] // blocks).reshape([-1 if axis == dim else 1 for axis in range(len(shape))])
    return loudness


def routed_block(rng, own, number, rows, count, top, bound, slope):
    order = jax.random.permutation(rng, count)
    heavy_load, common = shares(count, rows * top, bound, slope, True), shares(count, rows * top, bound, slope, False)
    places = jnp.arange(count)

    def named(sizes, rotation):
        used = int((sizes > 0).sum())
        fixed = max(1, used // 4)
        passed = fixed + (places - fixed + rotation * (used - fixed)) % max(1, count - fixed)
        return jnp.zeros((count,), jnp.int32).at[order[jnp.where(places < fixed, places, passed)]].set(jnp.asarray(sizes, jnp.int32))

    sizes = jnp.where(number % 4 == 0, named(heavy_load, number // 4), named(common, number - number // 4 - 1))
    mixed = jax.random.permutation(jax.random.fold_in(own, 3), count)
    donor, receiver = mixed[0:count // 2 * 2:2], mixed[1:count // 2 * 2:2]
    margin = jnp.minimum(sizes[donor] - 1, bound - sizes[receiver]) // 2
    margin = jnp.where((donor == order[0]) | (receiver == order[0]) | (sizes[receiver] == 0), 0, jnp.maximum(margin, 0))
    passed = jax.random.randint(jax.random.fold_in(own, 4), (count // 2,), 0, 1 << 20) % (margin + 1)
    sizes = sizes.at[donor].add(-passed).at[receiver].add(passed)
    items = jnp.searchsorted(jnp.cumsum(sizes), jnp.arange(rows * top), side="right").astype(jnp.int32)
    grid = items.reshape(top, rows).T
    grid = grid[jax.random.permutation(jax.random.fold_in(own, 1), rows)]
    rotation = jax.random.randint(jax.random.fold_in(own, 2), (rows, 1), 0, top)
    return jnp.take_along_axis(grid, (jnp.arange(top)[None, :] + rotation) % top, axis=1)


def shares(number_of, total, most, slope, full):
    loads = [(1 << 20) // math.isqrt(grade ** slope) + 1 for grade in range(1, number_of + 1)]
    largest = most if full else min(most, max(-(-total // number_of), total * loads[0] // sum(loads)))
    least = 1 if total - largest >= number_of - 1 else 0
    counts, surplus = [largest] + [least] * (number_of - 1), total - largest - least * (number_of - 1)
    while surplus > 0:
        candidates = [i for i in range(1, number_of) if counts[i] < largest] or [i for i in range(1, number_of) if counts[i] < most]
        pool, remaining = sum([loads[i] for i in candidates]), surplus
        for i in candidates:
            extra = min(most - counts[i], max(1, remaining * loads[i] // pool), surplus)
            counts[i] = counts[i] + extra
            surplus = surplus - extra
    return np.array(counts)


def centred(stream_key, dims, spread, reach, shards=(), held_as=jnp.bfloat16):
    values = spread * jax.random.normal(stream_key, dims, jnp.float32)
    if shards:
        values = values * block_scale(stream_key, dims, shards, -0.22, 0.18)
    return jnp.clip(values, -reach, reach).astype(held_as)


def noise_with(stream_key, shape, deviation, most, cuts, heavy, dtype=jnp.bfloat16):
    entries = deviation * jax.random.normal(stream_key, shape, jnp.float32)
    if cuts:
        entries = entries * block_scale(stream_key, shape, cuts, -0.22, 0.18)
    return jnp.clip(spiked(entries, jax.random.fold_in(stream_key, 3), *heavy), -most, most).astype(dtype)


def setup_inputs(seed: int = 0) -> dict:
    seeds = jax.random.split(jax.random.key(seed), 7)
    parent_slab = centred(seeds[0], (SLAB, PAR), 1.0, 6.0, ((0, 16), (1, 16)), jnp.float32)
    panel = noise_with(seeds[1], (N_CHILD, NU, B), NU ** -0.5, 0.0625, ((0, 2), (1, 8)), (1, 2, 8, 2.0), jnp.float32)
    slab_panel = noise_with(seeds[2], (N_CHILD, SLAB, B), SLAB ** -0.5, 0.15625, ((0, 2), (1, 16)), (1, 2, 16, 2.0), jnp.float32)
    diag_inverse = centred(seeds[3], (N_CHILD, B, B), 1.0, 6.0, ((0, 2), (1, 16), (2, 8)), jnp.float32)
    tile_rows = draw_tile_rows(jax.random.fold_in(seeds[6], 71), 0)
    tile_owner_keys = jax.random.split(jax.random.fold_in(seeds[5], 1), N_CHILD * NT // TILE_DEV)
    tile_owner_turns = jax.random.permutation(jax.random.fold_in(seeds[5], 3), N_CHILD * NT // TILE_DEV)
    tile_owner = jax.vmap(lambda own, number: routed_block(jax.random.fold_in(seeds[5], 2), own, number, TILE_DEV, N_CHILD * N_ROW, 1, CAP, 2))(tile_owner_keys, tile_owner_turns).reshape((N_CHILD, NT, 1))
    return dict(parent_slab=parent_slab, panel=panel, slab_panel=slab_panel, diag_inverse=diag_inverse, tile_rows=tile_rows, tile_owner=tile_owner)


def reference(parent_slab, panel, slab_panel, diag_inverse, tile_rows, tile_owner):
    block_cols = PAR // (N_CHILD * N_ROW)
    slab_parts = []
    diag_parts = []
    for child_id in range(N_CHILD):
        offsets = tile_rows[child_id]
        present = offsets >= 0
        row_index = tile_owner[child_id, :, 0][:, None] * block_cols + offsets
        flat_cols = jnp.where(present, row_index, 0).reshape(-1).astype(jnp.int32)
        columns = jnp.take(parent_slab, flat_cols, axis=1) * present.reshape(-1).astype(jnp.float32)[None, :]
        slab_part = -jnp.dot(columns, panel[child_id], precision=lax.Precision.HIGHEST, preferred_element_type=jnp.float32)
        diag_part = diag_inverse[child_id] - jnp.dot(slab_panel[child_id].T, slab_part, precision=lax.Precision.HIGHEST, preferred_element_type=jnp.float32)
        slab_parts.append(slab_part)
        diag_parts.append(diag_part)
    return jnp.stack(slab_parts), jnp.stack(diag_parts)
```

```python
import jax
import jax.numpy as jnp
from jax import lax
from jax.experimental import pallas as pl
from jax.experimental.pallas import tpu as pltpu
from jax.sharding import PartitionSpec as P

CAP = 2
VMEM_LIMIT = 48 << 20


def split(value):
    high = value.astype(jnp.bfloat16)
    low = (value - high.astype(jnp.float32)).astype(jnp.bfloat16)
    return high, low


def dot(left, right, contract=((1,), (0,))):
    return lax.dot_general(left, right, (contract, ((), ())), preferred_element_type=jnp.float32)


def gather_kernel(owner, me, rows, slab, out, parts, tiles, slots):
    slab_rows, width = slab.shape
    blocks, count = owner.shape
    high, low = split(slab[...])
    parts[0:slab_rows, :] = high
    parts[slab_rows:, :] = low
    mine = me[0]

    def block_scan(block, found):
        def tile_scan(tile, carry):
            found, rank = carry
            hit = (owner[block, tile] == mine).astype(jnp.int32)
            tiles[found] = block * count + tile
            slots[found] = block * CAP + rank
            return found + hit, rank + hit

        return lax.fori_loop(0, count, tile_scan, (found, 0))[0]

    found = lax.fori_loop(0, blocks, block_scan, 0)
    tiles[found] = 0
    chunk = width // 5

    def pair(step, carry):
        first = 2 * step
        second = first + 1
        columns = jnp.concatenate([rows[pl.ds(tiles[first], 1), :], rows[pl.ds(tiles[second], 1), :]], axis=1)
        total = jnp.zeros((2 * slab_rows, columns.shape[1]), jnp.float32)
        for begin in range(0, width, chunk):
            places = lax.broadcasted_iota(jnp.int32, (chunk, columns.shape[1]), 0) + begin
            picks = jnp.where(places == columns, 1.0, 0.0).astype(jnp.bfloat16)
            total += dot(parts[:, begin : begin + chunk], picks)
        total = total[:slab_rows] + total[slab_rows:]
        half = columns.shape[1] // 2
        out[slots[first]] = total[:, :half]

        @pl.when(second < found)
        def _():
            out[slots[second]] = total[:, half:]

        return carry

    lax.fori_loop(0, (found + 1) // 2, pair, 0)


def gather(parent_slab, rows, owner, me):
    slab_rows, width = parent_slab.shape
    blocks, count = owner.shape
    tile_len = rows.shape[1]
    smem = pl.BlockSpec(memory_space=pltpu.SMEM)
    vmem = pl.BlockSpec(memory_space=pltpu.VMEM)
    return pl.pallas_call(
        gather_kernel,
        out_shape=jax.ShapeDtypeStruct((blocks * CAP, slab_rows, tile_len), jnp.float32),
        in_specs=[smem, smem, vmem, vmem],
        out_specs=vmem,
        scratch_shapes=[
            pltpu.VMEM((2 * slab_rows, width), jnp.bfloat16),
            pltpu.SMEM((blocks * CAP + 8,), jnp.int32),
            pltpu.SMEM((blocks * CAP + 8,), jnp.int32),
        ],
        compiler_params=pltpu.CompilerParams(vmem_limit_bytes=VMEM_LIMIT),
    )(owner, me, rows, parent_slab)


def product_kernel(owner, me, arrived, panel, out, total):
    step = pl.program_id(0)
    count = owner.shape[1]
    mine = me[0]

    def slot_of(tile):
        own = owner[mine, tile]

        def earlier(other, rank):
            return rank + jnp.where((owner[mine, other] == own) & (other < tile), 1, 0)

        return own * CAP + lax.fori_loop(0, count, earlier, 0)

    left = jnp.concatenate([arrived[slot_of(2 * step)], arrived[slot_of(2 * step + 1)]], axis=1)
    left_high, left_low = split(left)
    right_high, right_low = split(panel[...])
    term = dot(left_high, right_high) + dot(left_high, right_low) + dot(left_low, right_high)

    @pl.when(step == 0)
    def _():
        total[...] = -term

    @pl.when(step > 0)
    def _():
        total[...] -= term

    @pl.when(step == pl.num_programs(0) - 1)
    def _():
        width = out.shape[2]
        for block in range(out.shape[0]):
            out[block] = total[:, block * width : (block + 1) * width]


def product(arrived, panel, owner, me, blocks):
    slots, slab_rows, tile_len = arrived.shape
    panel_rows, width = panel.shape
    smem = pl.BlockSpec(memory_space=pltpu.SMEM)
    out_shape = (blocks, slab_rows, width // blocks)
    return pl.pallas_call(
        product_kernel,
        grid=(panel_rows // (2 * tile_len),),
        out_shape=jax.ShapeDtypeStruct(out_shape, jnp.float32),
        in_specs=[
            smem,
            smem,
            pl.BlockSpec(arrived.shape, lambda i: (0, 0, 0)),
            pl.BlockSpec((2 * tile_len, width), lambda i: (i, 0)),
        ],
        out_specs=pl.BlockSpec(out_shape, lambda i: (0, 0, 0)),
        scratch_shapes=[pltpu.VMEM((slab_rows, width), jnp.float32)],
        compiler_params=pltpu.CompilerParams(vmem_limit_bytes=VMEM_LIMIT),
    )(owner, me, arrived, panel)


def diag_kernel(terms, slab_panel, inverse, out):
    total = jnp.sum(terms[...], axis=0)
    inverse[...] = total
    right_high, right_low = split(total)
    left_high, left_low = split(slab_panel[...])
    both = ((0,), (0,))
    result = dot(left_high, right_high, both) + dot(left_high, right_low, both) + dot(left_low, right_high, both)
    out[...] = result.reshape(out.shape)


def diag_terms(terms, slab_panel, blocks):
    _, slab_rows, width = terms.shape
    rows = slab_panel.shape[1]
    vmem = pl.BlockSpec(memory_space=pltpu.VMEM)
    return pl.pallas_call(
        diag_kernel,
        out_shape=(
            jax.ShapeDtypeStruct((slab_rows, width), jnp.float32),
            jax.ShapeDtypeStruct((blocks, rows // blocks, width), jnp.float32),
        ),
        in_specs=[vmem, vmem],
        out_specs=(vmem, vmem),
        compiler_params=pltpu.CompilerParams(vmem_limit_bytes=VMEM_LIMIT),
    )(terms, slab_panel)


def local(parent_slab, panel, slab_panel, diag_inverse, tile_rows, tile_owner):
    row_count, col_count = lax.axis_size("row"), lax.axis_size("col")
    group_size = lax.axis_size("child") * row_count
    me = (lax.axis_index("child") * row_count + lax.axis_index("row")).astype(jnp.int32).reshape(1)
    owner = tile_owner.reshape(group_size, -1)
    rows = tile_rows.reshape(-1, tile_rows.shape[2])
    columns = gather(parent_slab, rows, owner, me)
    arrived = lax.all_to_all(columns, ("child", "row"), split_axis=0, concat_axis=0, tiled=True)
    partial = product(arrived, panel[0], owner, me, row_count)
    terms = lax.all_to_all(partial, "row", split_axis=0, concat_axis=0, tiled=True)
    slab_inverse, parts = diag_terms(terms, slab_panel[0], col_count)
    reduced = lax.all_to_all(parts, "col", split_axis=0, concat_axis=0, tiled=True)
    diag_block = diag_inverse[0] - jnp.sum(reduced, axis=0)
    return slab_inverse[None], diag_block[None]


def solution(mesh):
    in_specs = (
        P("col", ("child", "row")),
        P("child", "row", None),
        P("child", "col", None),
        P("child", "col", "row"),
        P(),
        P(),
    )
    out_specs = (P("child", "col", "row"), P("child", "col", "row"))
    return jax.shard_map(local, mesh=mesh, in_specs=in_specs, out_specs=out_specs, check_vma=False)
```

```python
import functools

import jax
import jax.numpy as jnp
from jax import lax
from jax.experimental import pallas as pl
from jax.experimental.pallas import tpu as pltpu
from jax.sharding import PartitionSpec as P

CAP = 2
VMEM_LIMIT = 48 << 20


def split(value):
    high = value.astype(jnp.bfloat16)
    low = (value - high.astype(jnp.float32)).astype(jnp.bfloat16)
    return high, low


def dot(left, right, contract=((1,), (0,))):
    return lax.dot_general(left, right, (contract, ((), ())), preferred_element_type=jnp.float32)


def rank_of(owner, block, tile, count):
    own = owner[block, tile]

    def earlier(other, rank):
        return rank + jnp.where(owner[block, other] == own, 1, 0)

    return lax.fori_loop(0, tile, earlier, 0)


def gather_kernel(wanted, owner, me, rows, slab, out, parts, tiles, slots):
    slab_rows, width = slab.shape
    blocks, count = owner.shape
    high, low = split(slab[...])
    parts[0:slab_rows, :] = high
    parts[slab_rows:, :] = low
    mine = me[0]

    def block_scan(block, found):
        def tile_scan(tile, carry):
            found, rank = carry
            hit = owner[block, tile] == mine
            tiles[found] = block * count + tile
            slots[found] = block
            return found + (hit & (rank == wanted)).astype(jnp.int32), rank + hit.astype(jnp.int32)

        return lax.fori_loop(0, count, tile_scan, (found, 0))[0]

    found = lax.fori_loop(0, blocks, block_scan, 0)
    tiles[found] = 0
    chunk = width // 5

    def pair(step, carry):
        first = 2 * step
        second = first + 1
        columns = jnp.concatenate([rows[pl.ds(tiles[first], 1), :], rows[pl.ds(tiles[second], 1), :]], axis=1)
        total = jnp.zeros((2 * slab_rows, columns.shape[1]), jnp.float32)
        for begin in range(0, width, chunk):
            places = lax.broadcasted_iota(jnp.int32, (chunk, columns.shape[1]), 0) + begin
            picks = jnp.where(places == columns, 1.0, 0.0).astype(jnp.bfloat16)
            total += dot(parts[:, begin : begin + chunk], picks)
        total = total[:slab_rows] + total[slab_rows:]
        half = columns.shape[1] // 2
        out[slots[first]] = total[:, :half]

        @pl.when(second < found)
        def _():
            out[slots[second]] = total[:, half:]

        return carry

    lax.fori_loop(0, (found + 1) // 2, pair, 0)


def gather(wanted, parent_slab, rows, owner, me):
    slab_rows, width = parent_slab.shape
    blocks = owner.shape[0]
    tile_len = rows.shape[1]
    smem = pl.BlockSpec(memory_space=pltpu.SMEM)
    vmem = pl.BlockSpec(memory_space=pltpu.VMEM)
    return pl.pallas_call(
        functools.partial(gather_kernel, wanted),
        out_shape=jax.ShapeDtypeStruct((blocks, slab_rows, tile_len), jnp.float32),
        in_specs=[smem, smem, vmem, vmem],
        out_specs=vmem,
        scratch_shapes=[
            pltpu.VMEM((2 * slab_rows, width), jnp.bfloat16),
            pltpu.SMEM((blocks + 8,), jnp.int32),
            pltpu.SMEM((blocks + 8,), jnp.int32),
        ],
        compiler_params=pltpu.CompilerParams(vmem_limit_bytes=VMEM_LIMIT),
        cost_estimate=pl.CostEstimate(flops=blocks * 4 * slab_rows * width * tile_len, bytes_accessed=8 << 20, transcendentals=0),
    )(owner, me, rows, parent_slab)


def triple(left, right):
    left_high, left_low = split(left)
    right_high, right_low = split(right)
    return dot(
        jnp.concatenate([left_high, left_high, left_low], axis=1),
        jnp.concatenate([right_high, right_low, right_high], axis=0),
    )


def first_kernel(owner, me, arrived, panel, total):
    step = pl.program_id(0)
    count = owner.shape[1]
    mine = me[0]

    def part(tile):
        return jnp.where(rank_of(owner, mine, tile, count) == 0, arrived[owner[mine, tile]], 0.0)

    left = jnp.concatenate([part(2 * step), part(2 * step + 1)], axis=1)
    term = triple(left, panel[...])

    @pl.when(step == 0)
    def _():
        total[...] = -term

    @pl.when(step > 0)
    def _():
        total[...] -= term


def first_product(arrived, panel, owner, me):
    _, slab_rows, tile_len = arrived.shape
    panel_rows, width = panel.shape
    smem = pl.BlockSpec(memory_space=pltpu.SMEM)
    return pl.pallas_call(
        first_kernel,
        grid=(panel_rows // (2 * tile_len),),
        out_shape=jax.ShapeDtypeStruct((slab_rows, width), jnp.float32),
        in_specs=[
            smem,
            smem,
            pl.BlockSpec(arrived.shape, lambda i: (0, 0, 0)),
            pl.BlockSpec((2 * tile_len, width), lambda i: (i, 0)),
        ],
        out_specs=pl.BlockSpec((slab_rows, width), lambda i: (0, 0)),
        compiler_params=pltpu.CompilerParams(vmem_limit_bytes=VMEM_LIMIT),
        cost_estimate=pl.CostEstimate(flops=6 * slab_rows * width * panel_rows, bytes_accessed=16 << 20, transcendentals=0),
    )(owner, me, arrived, panel)


def second_kernel(groups, owner, me, first, arrived, panel, out, total, held, tiles, sems):
    count = owner.shape[1]
    tile_len = held.shape[1]
    mine = me[0]

    def copy(tile, place):
        source = panel.at[pl.ds(pl.multiple_of(tile * tile_len, tile_len), tile_len), :]
        return pltpu.make_async_copy(source, held.at[place], sems.at[place])

    def scan(tile, found):
        hit = rank_of(owner, mine, tile, count) == 1

        @pl.when(hit)
        def _():
            tiles[found] = tile
            copy(tile, found).start()

        return found + hit.astype(jnp.int32)

    found = lax.fori_loop(0, count, scan, 0)
    total[...] = first[...]

    def step(place, carry):
        tile = tiles[place]
        copy(tile, place).wait()
        total[...] -= triple(arrived[lax.rem(owner[mine, tile], groups)], held[place])
        return carry

    lax.fori_loop(0, found, step, 0)
    width = out.shape[2]
    for block in range(out.shape[0]):
        out[block] = total[:, block * width : (block + 1) * width]


def second_product(first, arrived, panel, owner, me, blocks):
    groups, slab_rows, tile_len = arrived.shape
    width = panel.shape[1]
    most = owner.shape[1] // CAP
    smem = pl.BlockSpec(memory_space=pltpu.SMEM)
    vmem = pl.BlockSpec(memory_space=pltpu.VMEM)
    return pl.pallas_call(
        functools.partial(second_kernel, groups),
        out_shape=jax.ShapeDtypeStruct((blocks, slab_rows, width // blocks), jnp.float32),
        in_specs=[smem, smem, vmem, vmem, pl.BlockSpec(memory_space=pl.ANY)],
        out_specs=vmem,
        scratch_shapes=[
            pltpu.VMEM((slab_rows, width), jnp.float32),
            pltpu.VMEM((most, tile_len, width), jnp.float32),
            pltpu.SMEM((most + 8,), jnp.int32),
            pltpu.SemaphoreType.DMA((most,)),
        ],
        compiler_params=pltpu.CompilerParams(vmem_limit_bytes=VMEM_LIMIT),
    )(owner, me, first, arrived, panel)


def diag_kernel(terms, slab_panel, inverse, out):
    total = jnp.sum(terms[...], axis=0)
    inverse[...] = total
    right_high, right_low = split(total)
    left_high, left_low = split(slab_panel[...])
    both = ((0,), (0,))
    result = dot(left_high, right_high, both) + dot(left_high, right_low, both) + dot(left_low, right_high, both)
    out[...] = result.reshape(out.shape)


def diag_terms(terms, slab_panel, blocks):
    _, slab_rows, width = terms.shape
    rows = slab_panel.shape[1]
    vmem = pl.BlockSpec(memory_space=pltpu.VMEM)
    return pl.pallas_call(
        diag_kernel,
        out_shape=(
            jax.ShapeDtypeStruct((slab_rows, width), jnp.float32),
            jax.ShapeDtypeStruct((blocks, rows // blocks, width), jnp.float32),
        ),
        in_specs=[vmem, vmem],
        out_specs=(vmem, vmem),
        compiler_params=pltpu.CompilerParams(vmem_limit_bytes=VMEM_LIMIT),
    )(terms, slab_panel)


def local(parent_slab, panel, slab_panel, diag_inverse, tile_rows, tile_owner):
    row_count, col_count = lax.axis_size("row"), lax.axis_size("col")
    group_size = lax.axis_size("child") * row_count
    child = lax.axis_index("child")
    me = (child * row_count + lax.axis_index("row")).astype(jnp.int32).reshape(1)
    owner = tile_owner.reshape(group_size, -1)
    rows = tile_rows.reshape(-1, tile_rows.shape[2])
    first_columns = gather(0, parent_slab, rows, owner, me)
    first_arrived = lax.all_to_all(first_columns, ("child", "row"), split_axis=0, concat_axis=0, tiled=True)
    second_columns = gather(1, parent_slab, rows, owner, me)
    own = lax.dynamic_slice_in_dim(second_columns, child * row_count, row_count, 0)
    other = lax.dynamic_slice_in_dim(second_columns, (1 - child) * row_count, row_count, 0)
    passed = lax.ppermute(other, "child", [(0, 1), (1, 0)])
    twice = jnp.sum((owner[:, :, None] == jnp.arange(group_size)).astype(jnp.int32), axis=1) > 1
    mine = lax.dynamic_slice(twice, (child * row_count, me[0]), (row_count, 1))
    merged = jnp.where(mine[:, :, None], own, passed)
    single = ~jnp.any(twice[:, :row_count] & twice[:, row_count:])

    def merged_sends(first_arrived, second_columns, merged):
        arrived = lax.all_to_all(merged, "row", split_axis=0, concat_axis=0, tiled=True)
        first = first_product(first_arrived, panel[0], owner, me)
        return second_product(first, arrived, panel[0], owner, me, row_count)

    def all_sends(first_arrived, second_columns, merged):
        arrived = lax.all_to_all(second_columns, ("child", "row"), split_axis=0, concat_axis=0, tiled=True)
        first = first_product(first_arrived, panel[0], owner, me)
        return second_product(first, arrived, panel[0], owner, me, row_count)

    partial = lax.cond(single, merged_sends, all_sends, first_arrived, second_columns, merged)
    terms = lax.all_to_all(partial, "row", split_axis=0, concat_axis=0, tiled=True)
    slab_inverse, parts = diag_terms(terms, slab_panel[0], col_count)
    reduced = lax.all_to_all(parts, "col", split_axis=0, concat_axis=0, tiled=True)
    diag_block = diag_inverse[0] - jnp.sum(reduced, axis=0)
    return slab_inverse[None], diag_block[None]


def solution(mesh):
    in_specs = (
        P("col", ("child", "row")),
        P("child", "row", None),
        P("child", "col", None),
        P("child", "col", "row"),
        P(),
        P(),
    )
    out_specs = (P("child", "col", "row"), P("child", "col", "row"))
    return jax.shard_map(local, mesh=mesh, in_specs=in_specs, out_specs=out_specs, check_vma=False)
```

```python
import functools

import jax
import jax.numpy as jnp
from jax import lax
from jax.experimental import pallas as pl
from jax.experimental.pallas import tpu as pltpu
from jax.sharding import PartitionSpec as P

CAP = 2
VMEM_LIMIT = 48 << 20
CHUNKS = 5


def split(value):
    high = value.astype(jnp.bfloat16)
    low = (value - high.astype(jnp.float32)).astype(jnp.bfloat16)
    return high, low


def dot(left, right, contract=((1,), (0,))):
    return lax.dot_general(left, right, (contract, ((), ())), preferred_element_type=jnp.float32)


def rank_of(owner, tile, first):
    own = owner[tile]

    def earlier(other, rank):
        return rank + jnp.where(owner[other] == own, 1, 0)

    return lax.fori_loop(first, tile, earlier, 0)


def gather_kernel(wanted, count, visit, owner, me, rows_in, slab_in, *refs):
    out, parts, slab, rows, tiles, slots, sems = refs[-7:]
    slab_rows, width = parts.shape[0] // 2, parts.shape[1]
    chunks, _, chunk = slab.shape
    copies = [pltpu.make_async_copy(rows_in, rows, sems.at[chunks])]
    for place in range(chunks):
        source = slab_in.at[:, place * chunk : (place + 1) * chunk]
        copies.append(pltpu.make_async_copy(source, slab.at[place], sems.at[place]))
    for copy in copies:
        copy.start()
    mine = me[0]

    def block_scan(slot, found):
        begin = visit(slot, mine) * count
        first, second = jnp.int32(-1), jnp.int32(-1)
        for tile in reversed(range(count)):
            hit = owner[begin + tile] == mine
            second = jnp.where(hit, first, second)
            first = jnp.where(hit, begin + tile, first)
        tile = second if wanted else first
        tiles[found] = jnp.maximum(tile, 0)
        slots[found] = slot
        return found + jnp.where(tile >= 0, 1, 0)

    found = lax.fori_loop(0, out.shape[0], block_scan, 0)
    tiles[found] = 0
    for copy in copies:
        copy.wait()

    @pl.when(found > 0)
    def _():
        for place in range(chunks):
            high, low = split(slab[place])
            parts[0:slab_rows, place * chunk : (place + 1) * chunk] = high
            parts[slab_rows:, place * chunk : (place + 1) * chunk] = low

    def pair(step, carry):
        first = 2 * step
        second = first + 1
        columns = jnp.concatenate([rows[pl.ds(tiles[first], 1), :], rows[pl.ds(tiles[second], 1), :]], axis=1)
        total = jnp.zeros((2 * slab_rows, columns.shape[1]), jnp.float32)
        for begin in range(0, width, chunk):
            places = lax.broadcasted_iota(jnp.int32, (chunk, columns.shape[1]), 0) + begin
            picks = jnp.where(places == columns, 1.0, 0.0).astype(jnp.bfloat16)
            total += dot(parts[:, begin : begin + chunk], picks)
        total = total[:slab_rows] + total[slab_rows:]
        half = columns.shape[1] // 2
        out[slots[first]] = total[:, :half]

        @pl.when(second < found)
        def _():
            out[slots[second]] = total[:, half:]

        return carry

    lax.fori_loop(0, (found + 1) // 2, pair, 0)


def gather(wanted, count, slots, visit, parent_slab, rows, owner, me, onto=None):
    slab_rows, width = parent_slab.shape
    tile_len = rows.shape[1]
    smem = pl.BlockSpec(memory_space=pltpu.SMEM)
    vmem = pl.BlockSpec(memory_space=pltpu.VMEM)
    hbm = pl.BlockSpec(memory_space=pl.ANY)
    given = [] if onto is None else [onto]
    return pl.pallas_call(
        functools.partial(gather_kernel, wanted, count, visit),
        out_shape=jax.ShapeDtypeStruct((slots, slab_rows, tile_len), jnp.float32),
        in_specs=[smem, smem, hbm, hbm] + [vmem] * len(given),
        out_specs=vmem,
        input_output_aliases={4: 0} if given else {},
        scratch_shapes=[
            pltpu.VMEM((2 * slab_rows, width), jnp.bfloat16),
            pltpu.VMEM((CHUNKS, slab_rows, width // CHUNKS), jnp.float32),
            pltpu.VMEM(rows.shape, jnp.int32),
            pltpu.SMEM((slots + 8,), jnp.int32),
            pltpu.SMEM((slots + 8,), jnp.int32),
            pltpu.SemaphoreType.DMA((CHUNKS + 1,)),
        ],
        compiler_params=pltpu.CompilerParams(vmem_limit_bytes=VMEM_LIMIT),
        cost_estimate=pl.CostEstimate(flops=slots * 4 * slab_rows * width * tile_len, bytes_accessed=8 << 20, transcendentals=0),
    )(owner, me, rows, parent_slab, *given)


def triple(left, right):
    left_high, left_low = split(left)
    right_high, right_low = split(right)
    return dot(
        jnp.concatenate([left_high, left_high, left_low], axis=1),
        jnp.concatenate([right_high, right_low, right_high], axis=0),
    )


def first_kernel(count, owner, me, arrived, panel, total):
    step = pl.program_id(0)
    begin = me[0] * count

    def part(tile):
        return jnp.where(rank_of(owner, tile, begin) == 0, arrived[owner[tile]], 0.0)

    left = jnp.concatenate([part(begin + 2 * step), part(begin + 2 * step + 1)], axis=1)
    term = triple(left, panel[...])

    @pl.when(step == 0)
    def _():
        total[...] = -term

    @pl.when(step > 0)
    def _():
        total[...] -= term


def first_product(arrived, panel, owner, me):
    _, slab_rows, tile_len = arrived.shape
    panel_rows, width = panel.shape
    count = panel_rows // tile_len
    smem = pl.BlockSpec(memory_space=pltpu.SMEM)
    return pl.pallas_call(
        functools.partial(first_kernel, count),
        grid=(count // 2,),
        out_shape=jax.ShapeDtypeStruct((slab_rows, width), jnp.float32),
        in_specs=[
            smem,
            smem,
            pl.BlockSpec(arrived.shape, lambda i: (0, 0, 0)),
            pl.BlockSpec((2 * tile_len, width), lambda i: (i, 0)),
        ],
        out_specs=pl.BlockSpec((slab_rows, width), lambda i: (0, 0)),
        compiler_params=pltpu.CompilerParams(vmem_limit_bytes=VMEM_LIMIT),
        cost_estimate=pl.CostEstimate(flops=6 * slab_rows * width * panel_rows, bytes_accessed=16 << 20, transcendentals=0),
    )(owner, me, arrived, panel)


def second_kernel(count, place_of, owner, me, first, *refs):
    *arrived, panel, out, total, held, tiles, sems = refs
    tile_len = held.shape[1]
    begin = me[0] * count

    def copy(tile, slot):
        source = panel.at[pl.ds(pl.multiple_of((tile - begin) * tile_len, tile_len), tile_len), :]
        return pltpu.make_async_copy(source, held.at[slot], sems.at[slot])

    def scan(tile, found):
        hit = rank_of(owner, tile, begin) == 1

        @pl.when(hit)
        def _():
            tiles[found] = tile
            copy(tile, found).start()

        return found + jnp.where(hit, 1, 0)

    found = lax.fori_loop(begin, begin + count, scan, 0)
    total[...] = first[...]

    def step(slot, carry):
        tile = tiles[slot]
        copy(tile, slot).wait()
        place = place_of(owner[tile], me[0])
        for index, ref in enumerate(arrived):

            @pl.when(place == index)
            def _():
                total[...] -= triple(ref[...], held[slot])

        return carry

    lax.fori_loop(0, found, step, 0)
    width = out.shape[2]
    for block in range(out.shape[0]):
        out[block] = total[:, block * width : (block + 1) * width]


def second_product(first, arrived, place_of, panel, owner, me, blocks):
    slab_rows, tile_len = arrived[0].shape
    panel_rows, width = panel.shape
    count = panel_rows // tile_len
    most = count // CAP
    smem = pl.BlockSpec(memory_space=pltpu.SMEM)
    vmem = pl.BlockSpec(memory_space=pltpu.VMEM)
    return pl.pallas_call(
        functools.partial(second_kernel, count, place_of),
        out_shape=jax.ShapeDtypeStruct((blocks, slab_rows, width // blocks), jnp.float32),
        in_specs=[smem, smem, vmem] + [vmem] * len(arrived) + [pl.BlockSpec(memory_space=pl.ANY)],
        out_specs=vmem,
        scratch_shapes=[
            pltpu.VMEM((slab_rows, width), jnp.float32),
            pltpu.VMEM((most, tile_len, width), jnp.float32),
            pltpu.SMEM((most + 8,), jnp.int32),
            pltpu.SemaphoreType.DMA((most,)),
        ],
        compiler_params=pltpu.CompilerParams(vmem_limit_bytes=VMEM_LIMIT),
    )(owner, me, first, *arrived, panel)


def diag_kernel(terms, slab_panel, inverse, out):
    total = jnp.sum(terms[...], axis=0)
    inverse[...] = total
    right_high, right_low = split(total)
    left_high, left_low = split(slab_panel[...])
    both = ((0,), (0,))
    result = dot(left_high, right_high, both) + dot(left_high, right_low, both) + dot(left_low, right_high, both)
    out[...] = result.reshape(out.shape)


def diag_terms(terms, slab_panel, blocks):
    _, slab_rows, width = terms.shape
    rows = slab_panel.shape[1]
    vmem = pl.BlockSpec(memory_space=pltpu.VMEM)
    return pl.pallas_call(
        diag_kernel,
        out_shape=(
            jax.ShapeDtypeStruct((slab_rows, width), jnp.float32),
            jax.ShapeDtypeStruct((blocks, rows // blocks, width), jnp.float32),
        ),
        in_specs=[vmem, vmem],
        out_specs=(vmem, vmem),
        compiler_params=pltpu.CompilerParams(vmem_limit_bytes=VMEM_LIMIT),
    )(terms, slab_panel)


def local(parent_slab, panel, slab_panel, diag_inverse, tile_rows, tile_owner):
    row_count, col_count = lax.axis_size("row"), lax.axis_size("col")
    group_size = lax.axis_size("child") * row_count
    me = (lax.axis_index("child") * row_count + lax.axis_index("row")).astype(jnp.int32).reshape(1)
    owner = tile_owner.reshape(-1)
    rows = tile_rows.reshape(-1, tile_rows.shape[2])
    count = owner.shape[0] // group_size

    def own_child(slot, mine):
        row = lax.rem(mine, row_count)
        return mine - row + lax.rem(row + slot, row_count)

    def other_child(slot, mine):
        return lax.rem(own_child(slot, mine) + row_count, group_size)

    first_columns = gather(0, count, group_size, lambda slot, mine: slot, parent_slab, rows, owner, me)
    after = lax.optimization_barrier((me, first_columns))[0]
    first_arrived = lax.all_to_all(first_columns, ("child", "row"), split_axis=0, concat_axis=0, tiled=True)
    passed = gather(1, count, row_count, other_child, parent_slab, rows, owner, after)
    passed = lax.ppermute(passed, "child", [(0, 1), (1, 0)])
    merged = gather(1, count, row_count, own_child, parent_slab, rows, owner, after, passed)
    second_arrived = [merged[0]]
    for step in range(1, row_count):
        route = [(row, (row + step) % row_count) for row in range(row_count)]
        second_arrived.append(lax.ppermute(merged[step], "row", route))
    first = first_product(first_arrived, panel[0], owner, lax.optimization_barrier((me, merged))[0])
    blocks = lax.optimization_barrier((owner, first_columns))[0].reshape(group_size, count)
    twice = jnp.sum((blocks[:, :, None] == jnp.arange(group_size)).astype(jnp.int32), axis=1) > 1
    single = ~jnp.any(twice[:, :row_count] & twice[:, row_count:])

    def merged_sends(first, *arrived):
        def place_of(own, mine):
            return lax.rem(mine - own + group_size, row_count)

        return second_product(first, arrived, place_of, panel[0], owner, me, row_count)

    def all_sends(first, *arrived):
        columns = gather(1, count, group_size, lambda slot, mine: slot, parent_slab, rows, owner, me)
        columns = lax.all_to_all(columns, ("child", "row"), split_axis=0, concat_axis=0, tiled=True)
        arrived = [columns[place] for place in range(group_size)]
        return second_product(first, arrived, lambda own, mine: own, panel[0], owner, me, row_count)

    partial = lax.cond(single, merged_sends, all_sends, first, *second_arrived)
    terms = lax.all_to_all(partial, "row", split_axis=0, concat_axis=0, tiled=True)
    slab_inverse, parts = diag_terms(terms, slab_panel[0], col_count)
    reduced = lax.all_to_all(parts, "col", split_axis=0, concat_axis=0, tiled=True)
    diag_block = diag_inverse[0] - jnp.sum(reduced, axis=0)
    return slab_inverse[None], diag_block[None]


def solution(mesh):
    in_specs = (
        P("col", ("child", "row")),
        P("child", "row", None),
        P("child", "col", None),
        P("child", "col", "row"),
        P(),
        P(),
    )
    out_specs = (P("child", "col", "row"), P("child", "col", "row"))
    return jax.shard_map(local, mesh=mesh, in_specs=in_specs, out_specs=out_specs, check_vma=False)
```

```python
import functools

import jax
import jax.numpy as jnp
from jax import lax
from jax.experimental import pallas as pl
from jax.experimental.pallas import tpu as pltpu
from jax.sharding import PartitionSpec as P

CAP = 2
VMEM_LIMIT = 48 << 20
CHUNKS = 5
LANES = 128
SUBLANES = 8


def split(value):
    high = value.astype(jnp.bfloat16)
    low = (value - high.astype(jnp.float32)).astype(jnp.bfloat16)
    return high, low


def dot(left, right, contract=((1,), (0,))):
    return lax.dot_general(left, right, (contract, ((), ())), preferred_element_type=jnp.float32)


def rank_of(owner, tile, first):
    own = owner[tile]

    def earlier(other, rank):
        return rank + jnp.where(owner[other] == own, 1, 0)

    return lax.fori_loop(first, tile, earlier, 0)


def gather_kernel(wanted, count, visit, halves, owner, me, rows_in, slab_in, *refs):
    outs, has, (parts, slab, rows, tiles, slots, sems) = refs[:halves], refs[halves], refs[halves + 1 :][:6]
    _, slab_rows, chunk = slab.shape
    tile_len = rows.shape[1]
    visits = has.shape[0]
    index_copy = pltpu.make_async_copy(rows_in, rows, sems.at[CHUNKS])
    index_copy.start()
    copies = []
    for place in range(CHUNKS):
        source = slab_in.at[:, place * chunk : (place + 1) * chunk]
        copies.append(pltpu.make_async_copy(source, slab.at[place], sems.at[place]))
        copies[place].start()
    mine = me[0]

    def block_scan(slot, found):
        begin = visit(slot, mine) * count
        first, second = jnp.int32(-1), jnp.int32(-1)
        for tile in reversed(range(count)):
            hit = owner[begin + tile] == mine
            second = jnp.where(hit, first, second)
            first = jnp.where(hit, begin + tile, first)
        tile = second if wanted else first
        tiles[found] = jnp.maximum(tile, 0)
        slots[found] = slot
        has[slot] = jnp.where(tile >= 0, 1, 0)
        return found + jnp.where(tile >= 0, 1, 0)

    found = lax.fori_loop(0, visits, block_scan, 0)
    for spare in range(2):
        tiles[found + spare] = 0
    index_copy.wait()

    if halves == 1:
        stage, out_sems = refs[-2:]

        def leave(index):
            return pltpu.make_async_copy(stage.at[index], outs[0].at[slots[index]], out_sems.at[index])

        def emit(index, value):
            stage[index] = value

            @pl.when(index < found)
            def _():
                leave(index).start()

    else:
        half = visits // halves

        def emit(index, value):
            for part, out in enumerate(outs):

                @pl.when((index < found) & (slots[index] // half == part))
                def _():
                    out[slots[index] - part * half] = value

    def arrive(place):
        copies[place].wait()
        high, low = split(slab[place])
        parts[0:slab_rows, place * chunk : (place + 1) * chunk] = high
        parts[slab_rows:, place * chunk : (place + 1) * chunk] = low

    def group(step, fresh):
        index = 3 * step
        columns = jnp.concatenate([rows[pl.ds(tiles[index + k], 1), :] for k in range(2)], axis=1)
        total = jnp.zeros((2 * slab_rows, 2 * tile_len), jnp.float32)
        lanes = rows[pl.ds(tiles[index + 2], 1), :]
        lane = jnp.broadcast_to(lanes & (LANES - 1), (SUBLANES, tile_len))
        strip = jnp.broadcast_to(lanes >> 7, (SUBLANES, tile_len))
        picked = [jnp.zeros((SUBLANES, tile_len), jnp.float32)] * (slab_rows // SUBLANES)
        for place in range(CHUNKS):
            begin = place * chunk
            if fresh:
                arrive(place)
            places = lax.broadcasted_iota(jnp.int32, (chunk, 2 * tile_len), 0) + begin
            picks = jnp.where(places == columns, 1.0, 0.0).astype(jnp.bfloat16)
            total += dot(parts[:, begin : begin + chunk], picks)
            for offset in range(0, chunk, LANES):
                inside = strip == (begin + offset) // LANES
                for band in range(slab_rows // SUBLANES):
                    values = slab[place, band * SUBLANES : (band + 1) * SUBLANES, offset : offset + LANES]
                    picked[band] = jnp.where(inside, jnp.take_along_axis(values, lane, axis=1), picked[band])
        total = total[:slab_rows] + total[slab_rows:]
        emit(index, total[:, :tile_len])
        emit(index + 1, total[:, tile_len:])
        emit(index + 2, jnp.concatenate(picked, axis=0))

    @pl.when(found > 0)
    def _():
        group(0, True)

    @pl.when(found == 0)
    def _():
        for copy in copies:
            copy.wait()

    def later(step, carry):
        group(step, False)
        return carry

    lax.fori_loop(1, (found + 2) // 3, later, 0)

    if halves == 1:

        def finish(index, carry):
            leave(index).wait()
            return carry

        lax.fori_loop(0, found, finish, 0)


def gather(wanted, count, visits, halves, visit, parent_slab, rows, owner, me):
    slab_rows, width = parent_slab.shape
    tile_len = rows.shape[1]
    smem = pl.BlockSpec(memory_space=pltpu.SMEM)
    vmem = pl.BlockSpec(memory_space=pltpu.VMEM)
    hbm = pl.BlockSpec(memory_space=pl.ANY)
    scratch = [
        pltpu.VMEM((2 * slab_rows, width), jnp.bfloat16),
        pltpu.VMEM((CHUNKS, slab_rows, width // CHUNKS), jnp.float32),
        pltpu.VMEM(rows.shape, jnp.int32),
        pltpu.SMEM((visits + 8,), jnp.int32),
        pltpu.SMEM((visits + 8,), jnp.int32),
        pltpu.SemaphoreType.DMA((CHUNKS + 1,)),
    ]
    if halves == 1:
        scratch += [pltpu.VMEM((visits + 2, slab_rows, tile_len), jnp.float32), pltpu.SemaphoreType.DMA((visits + 2,))]
    out = jax.ShapeDtypeStruct((visits // halves, slab_rows, tile_len), jnp.float32)
    return pl.pallas_call(
        functools.partial(gather_kernel, wanted, count, visit, halves),
        out_shape=(out,) * halves + (jax.ShapeDtypeStruct((visits,), jnp.int32),),
        in_specs=[smem, smem, hbm, hbm],
        out_specs=(hbm if halves == 1 else vmem,) * halves + (smem,),
        scratch_shapes=scratch,
        compiler_params=pltpu.CompilerParams(vmem_limit_bytes=VMEM_LIMIT),
        cost_estimate=pl.CostEstimate(flops=visits * 4 * slab_rows * width * tile_len, bytes_accessed=8 << 20, transcendentals=0),
    )(owner, me, rows, parent_slab)


def merge_kernel(has, own, passed, *outs):
    for slot, out in enumerate(outs):

        @pl.when(has[slot] > 0)
        def _():
            out[...] = own[slot]

        @pl.when(has[slot] == 0)
        def _():
            out[...] = passed[slot]


def merge(has, own, passed):
    smem = pl.BlockSpec(memory_space=pltpu.SMEM)
    vmem = pl.BlockSpec(memory_space=pltpu.VMEM)
    slots = own.shape[0]
    return pl.pallas_call(
        merge_kernel,
        out_shape=(jax.ShapeDtypeStruct(own.shape[1:], own.dtype),) * slots,
        in_specs=[smem, vmem, vmem],
        out_specs=(vmem,) * slots,
        compiler_params=pltpu.CompilerParams(vmem_limit_bytes=VMEM_LIMIT),
    )(has, own, passed)


def triple(left, right):
    left_high, left_low = split(left)
    right_high, right_low = split(right)
    return dot(
        jnp.concatenate([left_high, left_high, left_low], axis=1),
        jnp.concatenate([right_high, right_low, right_high], axis=0),
    )


def first_kernel(count, owner, me, arrived, panel_in, total, panel, sems):
    steps, depth, _ = panel.shape
    begin = me[0] * count
    copies = [
        pltpu.make_async_copy(panel_in.at[step * depth : (step + 1) * depth, :], panel.at[step], sems.at[step])
        for step in range(steps)
    ]
    for copy in copies:
        copy.start()

    def part(tile):
        return jnp.where(rank_of(owner, tile, begin) == 0, arrived[owner[tile]], 0.0)

    for step in range(steps):
        left = jnp.concatenate([part(begin + 2 * step), part(begin + 2 * step + 1)], axis=1)
        copies[step].wait()
        term = triple(left, panel[step])
        if step == 0:
            total[...] = -term
        else:
            total[...] -= term


def first_product(arrived, panel, owner, me):
    _, slab_rows, tile_len = arrived.shape
    panel_rows, width = panel.shape
    count = panel_rows // tile_len
    smem = pl.BlockSpec(memory_space=pltpu.SMEM)
    vmem = pl.BlockSpec(memory_space=pltpu.VMEM)
    return pl.pallas_call(
        functools.partial(first_kernel, count),
        out_shape=jax.ShapeDtypeStruct((slab_rows, width), jnp.float32),
        in_specs=[smem, smem, vmem, pl.BlockSpec(memory_space=pl.ANY)],
        out_specs=vmem,
        scratch_shapes=[
            pltpu.VMEM((count // 2, 2 * tile_len, width), jnp.float32),
            pltpu.SemaphoreType.DMA((count // 2,)),
        ],
        compiler_params=pltpu.CompilerParams(vmem_limit_bytes=VMEM_LIMIT),
        cost_estimate=pl.CostEstimate(flops=6 * slab_rows * width * panel_rows, bytes_accessed=16 << 20, transcendentals=0),
    )(owner, me, arrived, panel)


def second_kernel(count, place_of, owner, me, first, *refs):
    *arrived, panel, out, left, held, tiles, sems = refs
    tile_len = held.shape[0] // sems.shape[0]
    begin = me[0] * count
    width = out.shape[2]

    def copy(tile, slot):
        source = panel.at[pl.ds(pl.multiple_of((tile - begin) * tile_len, tile_len), tile_len), :]
        target = held.at[pl.ds(pl.multiple_of(slot * tile_len, tile_len), tile_len), :]
        return pltpu.make_async_copy(source, target, sems.at[slot])

    def look(tile, found):
        hit = rank_of(owner, tile, begin) == 1

        @pl.when(hit)
        def _():
            tiles[found] = tile
            copy(tile, found).start()

        return found + jnp.where(hit, 1, 0)

    found = lax.fori_loop(begin, begin + count, look, 0)

    @pl.when(lax.rem(found, 2) == 1)
    def _():
        left[:, tile_len:] = jnp.zeros_like(left[:, tile_len:])
        held[pl.ds(pl.multiple_of(found * tile_len, tile_len), tile_len), :] = jnp.zeros((tile_len, held.shape[1]), jnp.float32)

    def side(slot, begin_lane):
        tile = tiles[slot]
        place = place_of(owner[tile], me[0])
        for index, ref in enumerate(arrived):

            @pl.when(place == index)
            def _():
                left[:, begin_lane : begin_lane + tile_len] = ref[...]

        copy(tile, slot).wait()

    def pair(step):
        side(2 * step, 0)

        @pl.when(2 * step + 1 < found)
        def _():
            side(2 * step + 1, tile_len)

        rows = pl.ds(pl.multiple_of(2 * step * tile_len, 2 * tile_len), 2 * tile_len)
        return triple(left[...], held[rows, :])

    @pl.when(found > 0)
    def _():
        term = pair(0)
        for block in range(out.shape[0]):
            columns = slice(block * width, (block + 1) * width)
            out[block] = first[:, columns] - term[:, columns]

    @pl.when(found == 0)
    def _():
        for block in range(out.shape[0]):
            out[block] = first[:, block * width : (block + 1) * width]

    def later(step, carry):
        @pl.when(2 * step + 1 >= found)
        def _():
            left[:, tile_len:] = jnp.zeros_like(left[:, tile_len:])

        term = pair(step)
        for block in range(out.shape[0]):
            out[block] -= term[:, block * width : (block + 1) * width]
        return carry

    lax.fori_loop(1, (found + 1) // 2, later, 0)


def second_product(first, arrived, place_of, panel, owner, me, blocks):
    slab_rows, tile_len = arrived[0].shape
    panel_rows, width = panel.shape
    count = panel_rows // tile_len
    most = count // CAP
    smem = pl.BlockSpec(memory_space=pltpu.SMEM)
    vmem = pl.BlockSpec(memory_space=pltpu.VMEM)
    return pl.pallas_call(
        functools.partial(second_kernel, count, place_of),
        out_shape=jax.ShapeDtypeStruct((blocks, slab_rows, width // blocks), jnp.float32),
        in_specs=[smem, smem, vmem] + [vmem] * len(arrived) + [pl.BlockSpec(memory_space=pl.ANY)],
        out_specs=vmem,
        scratch_shapes=[
            pltpu.VMEM((slab_rows, 2 * tile_len), jnp.float32),
            pltpu.VMEM((most * tile_len, width), jnp.float32),
            pltpu.SMEM((most + 8,), jnp.int32),
            pltpu.SemaphoreType.DMA((most,)),
        ],
        compiler_params=pltpu.CompilerParams(vmem_limit_bytes=VMEM_LIMIT),
    )(owner, me, first, *arrived, panel)


def diag_kernel(terms, slab_panel, inverse, out):
    total = jnp.sum(terms[...], axis=0)
    inverse[...] = total
    right_high, right_low = split(total)
    left_high, left_low = split(slab_panel[...])
    both = ((0,), (0,))
    result = dot(left_high, right_high, both) + dot(left_high, right_low, both) + dot(left_low, right_high, both)
    out[...] = result.reshape(out.shape)


def diag_terms(terms, slab_panel, blocks):
    _, slab_rows, width = terms.shape
    rows = slab_panel.shape[1]
    vmem = pl.BlockSpec(memory_space=pltpu.VMEM)
    return pl.pallas_call(
        diag_kernel,
        out_shape=(
            jax.ShapeDtypeStruct((slab_rows, width), jnp.float32),
            jax.ShapeDtypeStruct((blocks, rows // blocks, width), jnp.float32),
        ),
        in_specs=[vmem, vmem],
        out_specs=(vmem, vmem),
        compiler_params=pltpu.CompilerParams(vmem_limit_bytes=VMEM_LIMIT),
    )(terms, slab_panel)


def local(parent_slab, panel, slab_panel, diag_inverse, tile_rows, tile_owner):
    row_count, col_count = lax.axis_size("row"), lax.axis_size("col")
    group_size = lax.axis_size("child") * row_count
    me = (lax.axis_index("child") * row_count + lax.axis_index("row")).astype(jnp.int32).reshape(1)
    owner = tile_owner.reshape(-1)
    rows = tile_rows.reshape(-1, tile_rows.shape[2])
    count = owner.shape[0] // group_size

    def by_child(slot, mine):
        row = lax.rem(mine, row_count)
        child = mine // row_count + slot // row_count
        return lax.rem(child * row_count + lax.rem(row + slot, row_count), group_size)

    first_columns, _ = gather(0, count, group_size, 1, lambda slot, mine: slot, parent_slab, rows, owner, me)
    after = lax.optimization_barrier((me, first_columns))[0]
    first_arrived = lax.all_to_all(first_columns, ("child", "row"), split_axis=0, concat_axis=0, tiled=True)
    own, other, has = gather(1, count, group_size, 2, by_child, parent_slab, rows, owner, after)
    passed = lax.ppermute(other, "child", [(0, 1), (1, 0)])
    merged = merge(has, own, passed)
    second_arrived = [merged[0]] + [None] * (row_count - 1)
    for step in sorted(range(1, row_count), key=lambda step: min(step, row_count - step)):
        route = [(row, (row + step) % row_count) for row in range(row_count)]
        second_arrived[step] = lax.ppermute(merged[step], "row", route)
    first = first_product(first_arrived, panel[0], owner, lax.optimization_barrier((me, *merged))[0])
    blocks = lax.optimization_barrier((owner, first_columns))[0].reshape(group_size, count)
    twice = jnp.sum((blocks[:, :, None] == jnp.arange(group_size)).astype(jnp.int32), axis=1) > 1
    single = ~jnp.any(twice[:, :row_count] & twice[:, row_count:])

    def merged_sends(first, *arrived):
        def place_of(own, mine):
            return lax.rem(mine - own + group_size, row_count)

        return second_product(first, arrived, place_of, panel[0], owner, me, row_count)

    def all_sends(first, *arrived):
        columns, _ = gather(1, count, group_size, 1, lambda slot, mine: slot, parent_slab, rows, owner, me)
        columns = lax.all_to_all(columns, ("child", "row"), split_axis=0, concat_axis=0, tiled=True)
        arrived = [columns[place] for place in range(group_size)]
        return second_product(first, arrived, lambda own, mine: own, panel[0], owner, me, row_count)

    partial = lax.cond(single, merged_sends, all_sends, first, *second_arrived)
    terms = lax.all_to_all(partial, "row", split_axis=0, concat_axis=0, tiled=True)
    slab_inverse, parts = diag_terms(terms, slab_panel[0], col_count)
    reduced = lax.all_to_all(parts, "col", split_axis=0, concat_axis=0, tiled=True)
    diag_block = diag_inverse[0] - jnp.sum(reduced, axis=0)
    return slab_inverse[None], diag_block[None]


def solution(mesh):
    in_specs = (
        P("col", ("child", "row")),
        P("child", "row", None),
        P("child", "col", None),
        P("child", "col", "row"),
        P(),
        P(),
    )
    out_specs = (P("child", "col", "row"), P("child", "col", "row"))
    return jax.shard_map(local, mesh=mesh, in_specs=in_specs, out_specs=out_specs, check_vma=False)
```

```python
import functools

import jax
import jax.numpy as jnp
from jax import lax
from jax.experimental import pallas as pl
from jax.experimental.pallas import tpu as pltpu
from jax.sharding import PartitionSpec as P

CAP = 2
VMEM_LIMIT = 48 << 20
CHUNKS = 5
LANES = 128
SUBLANES = 8


def split(value):
    high = value.astype(jnp.bfloat16)
    low = (value - high.astype(jnp.float32)).astype(jnp.bfloat16)
    return high, low


def dot(left, right, contract=((1,), (0,))):
    return lax.dot_general(left, right, (contract, ((), ())), preferred_element_type=jnp.float32)


def rank_of(owner, tile, first):
    own = owner[tile]

    def earlier(other, rank):
        return rank + jnp.where(owner[other] == own, 1, 0)

    return lax.fori_loop(first, tile, earlier, 0)


def device_in_group():
    return lax.axis_index("child") * lax.axis_size("row") + lax.axis_index("row")


def gather_kernel(wanted, count, visit, halves, after, owner_in, rows_in, slab_in, *refs):
    outs, has, (parts, slab, rows, owner, tiles, slots, sems) = refs[:halves], refs[halves], refs[halves + 1 :][:7]
    _, slab_rows, chunk = slab.shape
    tile_len = rows.shape[1]
    visits = has.shape[0]
    owner_copy = pltpu.make_async_copy(owner_in, owner, sems.at[CHUNKS + 1])
    owner_copy.start()
    index_copy = pltpu.make_async_copy(rows_in, rows, sems.at[CHUNKS])
    index_copy.start()
    copies = []
    for place in range(CHUNKS):
        source = slab_in.at[:, place * chunk : (place + 1) * chunk]
        copies.append(pltpu.make_async_copy(source, slab.at[place], sems.at[place]))
        copies[place].start()
    mine = device_in_group()
    owner_copy.wait()

    def block_scan(slot, found):
        begin = visit(slot, mine) * count
        first, second = jnp.int32(-1), jnp.int32(-1)
        for tile in reversed(range(count)):
            hit = owner[begin + tile] == mine
            second = jnp.where(hit, first, second)
            first = jnp.where(hit, begin + tile, first)
        tile = second if wanted else first
        tiles[found] = jnp.maximum(tile, 0)
        slots[found] = slot
        has[slot] = jnp.where(tile >= 0, 1, 0)
        return found + jnp.where(tile >= 0, 1, 0)

    found = lax.fori_loop(0, visits, block_scan, 0)
    for spare in range(2):
        tiles[found + spare] = 0
    index_copy.wait()

    if halves == 1:
        stage, out_sems = refs[-2:]

        def leave(index):
            return pltpu.make_async_copy(stage.at[index], outs[0].at[slots[index]], out_sems.at[index])

        def emit(index, value):
            stage[index] = value

            @pl.when(index < found)
            def _():
                leave(index).start()

    else:
        half = visits // halves

        def emit(index, value):
            for part, out in enumerate(outs):

                @pl.when((index < found) & (slots[index] // half == part))
                def _():
                    out[slots[index] - part * half] = value

    def arrive(place):
        copies[place].wait()
        high, low = split(slab[place])
        parts[0:slab_rows, place * chunk : (place + 1) * chunk] = high
        parts[slab_rows:, place * chunk : (place + 1) * chunk] = low

    def group(step, fresh):
        index = 3 * step
        columns = jnp.concatenate([rows[pl.ds(tiles[index + k], 1), :] for k in range(2)], axis=1)
        total = jnp.zeros((2 * slab_rows, 2 * tile_len), jnp.float32)
        lanes = rows[pl.ds(tiles[index + 2], 1), :]
        lane = jnp.broadcast_to(lanes & (LANES - 1), (SUBLANES, tile_len))
        strip = jnp.broadcast_to(lanes >> 7, (SUBLANES, tile_len))
        picked = [jnp.zeros((SUBLANES, tile_len), jnp.float32)] * (slab_rows // SUBLANES)
        for place in range(CHUNKS):
            begin = place * chunk
            if fresh:
                arrive(place)
            places = lax.broadcasted_iota(jnp.int32, (chunk, 2 * tile_len), 0) + begin
            picks = jnp.where(places == columns, 1.0, 0.0).astype(jnp.bfloat16)
            total += dot(parts[:, begin : begin + chunk], picks)
            for offset in range(0, chunk, LANES):
                inside = strip == (begin + offset) // LANES
                for band in range(slab_rows // SUBLANES):
                    values = slab[place, band * SUBLANES : (band + 1) * SUBLANES, offset : offset + LANES]
                    picked[band] = jnp.where(inside, jnp.take_along_axis(values, lane, axis=1), picked[band])
        total = total[:slab_rows] + total[slab_rows:]
        emit(index, total[:, :tile_len])
        emit(index + 1, total[:, tile_len:])
        emit(index + 2, jnp.concatenate(picked, axis=0))

    @pl.when(found > 0)
    def _():
        group(0, True)

    @pl.when(found == 0)
    def _():
        for copy in copies:
            copy.wait()

    def later(step, carry):
        group(step, False)
        return carry

    lax.fori_loop(1, (found + 2) // 3, later, 0)

    if halves == 1:

        def finish(index, carry):
            leave(index).wait()
            return carry

        lax.fori_loop(0, found, finish, 0)


def gather(wanted, count, visits, halves, visit, parent_slab, rows, owner, after):
    slab_rows, width = parent_slab.shape
    tile_len = rows.shape[1]
    smem = pl.BlockSpec(memory_space=pltpu.SMEM)
    vmem = pl.BlockSpec(memory_space=pltpu.VMEM)
    hbm = pl.BlockSpec(memory_space=pl.ANY)
    scratch = [
        pltpu.VMEM((2 * slab_rows, width), jnp.bfloat16),
        pltpu.VMEM((CHUNKS, slab_rows, width // CHUNKS), jnp.float32),
        pltpu.VMEM(rows.shape, jnp.int32),
        pltpu.SMEM(owner.shape, jnp.int32),
        pltpu.SMEM((visits + 8,), jnp.int32),
        pltpu.SMEM((visits + 8,), jnp.int32),
        pltpu.SemaphoreType.DMA((CHUNKS + 2,)),
    ]
    if halves == 1:
        scratch += [pltpu.VMEM((visits + 2, slab_rows, tile_len), jnp.float32), pltpu.SemaphoreType.DMA((visits + 2,))]
    out = jax.ShapeDtypeStruct((visits // halves, slab_rows, tile_len), jnp.float32)
    return pl.pallas_call(
        functools.partial(gather_kernel, wanted, count, visit, halves),
        out_shape=(out,) * halves + (jax.ShapeDtypeStruct((visits,), jnp.int32),),
        in_specs=[hbm, hbm, hbm, hbm],
        out_specs=(hbm if halves == 1 else vmem,) * halves + (smem,),
        scratch_shapes=scratch,
        compiler_params=pltpu.CompilerParams(vmem_limit_bytes=VMEM_LIMIT),
        cost_estimate=pl.CostEstimate(flops=visits * 4 * slab_rows * width * tile_len, bytes_accessed=8 << 20, transcendentals=0),
    )(after, owner, rows, parent_slab)


def merge_kernel(has, own, passed, *outs):
    for slot, out in enumerate(outs):

        @pl.when(has[slot] > 0)
        def _():
            out[...] = own[slot]

        @pl.when(has[slot] == 0)
        def _():
            out[...] = passed[slot]


def merge(has, own, passed):
    smem = pl.BlockSpec(memory_space=pltpu.SMEM)
    vmem = pl.BlockSpec(memory_space=pltpu.VMEM)
    slots = own.shape[0]
    return pl.pallas_call(
        merge_kernel,
        out_shape=(jax.ShapeDtypeStruct(own.shape[1:], own.dtype),) * slots,
        in_specs=[smem, vmem, vmem],
        out_specs=(vmem,) * slots,
        compiler_params=pltpu.CompilerParams(vmem_limit_bytes=VMEM_LIMIT),
    )(has, own, passed)


def triple(left, right):
    left_high, left_low = split(left)
    right_high, right_low = split(right)
    return dot(
        jnp.concatenate([left_high, left_high, left_low], axis=1),
        jnp.concatenate([right_high, right_low, right_high], axis=0),
    )


def first_kernel(count, owner, me, arrived, panel_in, total, panel, sems):
    steps, depth, _ = panel.shape
    begin = me[0] * count
    copies = [
        pltpu.make_async_copy(panel_in.at[step * depth : (step + 1) * depth, :], panel.at[step], sems.at[step])
        for step in range(steps)
    ]
    for copy in copies:
        copy.start()

    def part(tile):
        return jnp.where(rank_of(owner, tile, begin) == 0, arrived[owner[tile]], 0.0)

    for step in range(steps):
        left = jnp.concatenate([part(begin + 2 * step), part(begin + 2 * step + 1)], axis=1)
        copies[step].wait()
        term = triple(left, panel[step])
        if step == 0:
            total[...] = -term
        else:
            total[...] -= term


def first_product(arrived, panel, owner, me):
    _, slab_rows, tile_len = arrived.shape
    panel_rows, width = panel.shape
    count = panel_rows // tile_len
    smem = pl.BlockSpec(memory_space=pltpu.SMEM)
    vmem = pl.BlockSpec(memory_space=pltpu.VMEM)
    return pl.pallas_call(
        functools.partial(first_kernel, count),
        out_shape=jax.ShapeDtypeStruct((slab_rows, width), jnp.float32),
        in_specs=[smem, smem, vmem, pl.BlockSpec(memory_space=pl.ANY)],
        out_specs=vmem,
        scratch_shapes=[
            pltpu.VMEM((count // 2, 2 * tile_len, width), jnp.float32),
            pltpu.SemaphoreType.DMA((count // 2,)),
        ],
        compiler_params=pltpu.CompilerParams(vmem_limit_bytes=VMEM_LIMIT),
        cost_estimate=pl.CostEstimate(flops=6 * slab_rows * width * panel_rows, bytes_accessed=16 << 20, transcendentals=0),
    )(owner, me, arrived, panel)


def second_kernel(count, place_of, owner, first, *refs):
    *arrived, panel, out, left, held, tiles, sems = refs
    tile_len = held.shape[0] // sems.shape[0]
    mine = device_in_group()
    begin = mine * count
    width = out.shape[2]

    def copy(tile, slot):
        source = panel.at[pl.ds(pl.multiple_of((tile - begin) * tile_len, tile_len), tile_len), :]
        target = held.at[pl.ds(pl.multiple_of(slot * tile_len, tile_len), tile_len), :]
        return pltpu.make_async_copy(source, target, sems.at[slot])

    def look(tile, found):
        hit = rank_of(owner, tile, begin) == 1

        @pl.when(hit)
        def _():
            tiles[found] = tile
            copy(tile, found).start()

        return found + jnp.where(hit, 1, 0)

    found = lax.fori_loop(begin, begin + count, look, 0)

    @pl.when(lax.rem(found, 2) == 1)
    def _():
        left[:, tile_len:] = jnp.zeros_like(left[:, tile_len:])
        held[pl.ds(pl.multiple_of(found * tile_len, tile_len), tile_len), :] = jnp.zeros((tile_len, held.shape[1]), jnp.float32)

    def side(slot, begin_lane):
        tile = tiles[slot]
        place = place_of(owner[tile], mine)
        for index, ref in enumerate(arrived):

            @pl.when(place == index)
            def _():
                left[:, begin_lane : begin_lane + tile_len] = ref[...]

        copy(tile, slot).wait()

    def pair(step):
        side(2 * step, 0)

        @pl.when(2 * step + 1 < found)
        def _():
            side(2 * step + 1, tile_len)

        rows = pl.ds(pl.multiple_of(2 * step * tile_len, 2 * tile_len), 2 * tile_len)
        return triple(left[...], held[rows, :])

    @pl.when(found > 0)
    def _():
        term = pair(0)
        for block in range(out.shape[0]):
            columns = slice(block * width, (block + 1) * width)
            out[block] = first[:, columns] - term[:, columns]

    @pl.when(found == 0)
    def _():
        for block in range(out.shape[0]):
            out[block] = first[:, block * width : (block + 1) * width]

    def later(step, carry):
        @pl.when(2 * step + 1 >= found)
        def _():
            left[:, tile_len:] = jnp.zeros_like(left[:, tile_len:])

        term = pair(step)
        for block in range(out.shape[0]):
            out[block] -= term[:, block * width : (block + 1) * width]
        return carry

    lax.fori_loop(1, (found + 1) // 2, later, 0)


def second_product(first, arrived, place_of, panel, owner, me, blocks):
    slab_rows, tile_len = arrived[0].shape
    panel_rows, width = panel.shape
    count = panel_rows // tile_len
    most = count // CAP
    smem = pl.BlockSpec(memory_space=pltpu.SMEM)
    vmem = pl.BlockSpec(memory_space=pltpu.VMEM)
    return pl.pallas_call(
        functools.partial(second_kernel, count, place_of),
        out_shape=jax.ShapeDtypeStruct((blocks, slab_rows, width // blocks), jnp.float32),
        in_specs=[smem, vmem] + [vmem] * len(arrived) + [pl.BlockSpec(memory_space=pl.ANY)],
        out_specs=vmem,
        scratch_shapes=[
            pltpu.VMEM((slab_rows, 2 * tile_len), jnp.float32),
            pltpu.VMEM((most * tile_len, width), jnp.float32),
            pltpu.SMEM((most + 8,), jnp.int32),
            pltpu.SemaphoreType.DMA((most,)),
        ],
        compiler_params=pltpu.CompilerParams(vmem_limit_bytes=VMEM_LIMIT),
    )(owner, first, *arrived, panel)


def diag_kernel(terms, slab_panel, inverse, out):
    total = jnp.sum(terms[...], axis=0)
    inverse[...] = total
    right_high, right_low = split(total)
    left_high, left_low = split(slab_panel[...])
    both = ((0,), (0,))
    result = dot(left_high, right_high, both) + dot(left_high, right_low, both) + dot(left_low, right_high, both)
    out[...] = result.reshape(out.shape)


def diag_terms(terms, slab_panel, blocks):
    _, slab_rows, width = terms.shape
    rows = slab_panel.shape[1]
    vmem = pl.BlockSpec(memory_space=pltpu.VMEM)
    return pl.pallas_call(
        diag_kernel,
        out_shape=(
            jax.ShapeDtypeStruct((slab_rows, width), jnp.float32),
            jax.ShapeDtypeStruct((blocks, rows // blocks, width), jnp.float32),
        ),
        in_specs=[vmem, vmem],
        out_specs=(vmem, vmem),
        compiler_params=pltpu.CompilerParams(vmem_limit_bytes=VMEM_LIMIT),
    )(terms, slab_panel)


def local(parent_slab, panel, slab_panel, diag_inverse, tile_rows, tile_owner):
    row_count, col_count = lax.axis_size("row"), lax.axis_size("col")
    group_size = lax.axis_size("child") * row_count
    me = (lax.axis_index("child") * row_count + lax.axis_index("row")).astype(jnp.int32).reshape(1)
    owner = tile_owner.reshape(-1)
    rows = tile_rows.reshape(-1, tile_rows.shape[2])
    count = owner.shape[0] // group_size

    def by_child(slot, mine):
        row = lax.rem(mine, row_count)
        child = mine // row_count + slot // row_count
        return lax.rem(child * row_count + lax.rem(row + slot, row_count), group_size)

    first_columns, _ = gather(0, count, group_size, 1, lambda slot, mine: slot, parent_slab, rows, owner, me)
    after = lax.optimization_barrier((me, first_columns))[0]
    first_arrived = lax.all_to_all(first_columns, ("child", "row"), split_axis=0, concat_axis=0, tiled=True)
    own, other, has = gather(1, count, group_size, 2, by_child, parent_slab, rows, owner, after)
    passed = lax.ppermute(other, "child", [(0, 1), (1, 0)])
    merged = merge(has, own, passed)
    second_arrived = [merged[0]] + [None] * (row_count - 1)
    for step in sorted(range(1, row_count), key=lambda step: min(step, row_count - step)):
        route = [(row, (row + step) % row_count) for row in range(row_count)]
        second_arrived[step] = lax.ppermute(merged[step], "row", route)
    first = first_product(first_arrived, panel[0], owner, lax.optimization_barrier((me, *merged))[0])
    blocks = lax.optimization_barrier((owner, first_columns))[0].reshape(group_size, count)
    twice = jnp.sum((blocks[:, :, None] == jnp.arange(group_size)).astype(jnp.int32), axis=1) > 1
    single = ~jnp.any(twice[:, :row_count] & twice[:, row_count:])

    def merged_sends(first, *arrived):
        def place_of(own, mine):
            return lax.rem(mine - own + group_size, row_count)

        return second_product(first, arrived, place_of, panel[0], owner, me, row_count)

    def all_sends(first, *arrived):
        columns, _ = gather(1, count, group_size, 1, lambda slot, mine: slot, parent_slab, rows, owner, me)
        columns = lax.all_to_all(columns, ("child", "row"), split_axis=0, concat_axis=0, tiled=True)
        arrived = [columns[place] for place in range(group_size)]
        return second_product(first, arrived, lambda own, mine: own, panel[0], owner, me, row_count)

    partial = lax.cond(single, merged_sends, all_sends, first, *second_arrived)
    terms = lax.all_to_all(partial, "row", split_axis=0, concat_axis=0, tiled=True)
    slab_inverse, parts = diag_terms(terms, slab_panel[0], col_count)
    reduced = lax.all_to_all(parts, "col", split_axis=0, concat_axis=0, tiled=True)
    diag_block = diag_inverse[0] - jnp.sum(reduced, axis=0)
    return slab_inverse[None], diag_block[None]


def solution(mesh):
    in_specs = (
        P("col", ("child", "row")),
        P("child", "row", None),
        P("child", "col", None),
        P("child", "col", "row"),
        P(),
        P(),
    )
    out_specs = (P("child", "col", "row"), P("child", "col", "row"))
    return jax.shard_map(local, mesh=mesh, in_specs=in_specs, out_specs=out_specs, check_vma=False)
```

```python
import functools

import jax
import jax.numpy as jnp
from jax import lax
from jax.experimental import pallas as pl
from jax.experimental.pallas import tpu as pltpu
from jax.sharding import PartitionSpec as P

CAP = 2
VMEM_LIMIT = 48 << 20
CHUNKS = 5
LANES = 128
SUBLANES = 8


def split(value):
    high = value.astype(jnp.bfloat16)
    low = (value - high.astype(jnp.float32)).astype(jnp.bfloat16)
    return high, low


def dot(left, right, contract=((1,), (0,))):
    return lax.dot_general(left, right, (contract, ((), ())), preferred_element_type=jnp.float32)


def rank_of(owner, tile, first):
    own = owner[tile]

    def earlier(other, rank):
        return rank + jnp.where(owner[other] == own, 1, 0)

    return lax.fori_loop(first, tile, earlier, 0)


def device_in_group():
    return lax.axis_index("child") * lax.axis_size("row") + lax.axis_index("row")


def gather_kernel(wanted, count, visit, halves, after, owner_in, rows_in, slab_in, *refs):
    outs, has, (parts, slab, rows, owner, tiles, slots, sems) = refs[:halves], refs[halves], refs[halves + 1 :][:7]
    _, slab_rows, chunk = slab.shape
    tile_len = rows.shape[1]
    visits = has.shape[0]
    owner_copy = pltpu.make_async_copy(owner_in, owner, sems.at[CHUNKS + 1])
    owner_copy.start()
    index_copy = pltpu.make_async_copy(rows_in, rows, sems.at[CHUNKS])
    index_copy.start()
    copies = []
    for place in range(CHUNKS):
        source = slab_in.at[:, place * chunk : (place + 1) * chunk]
        copies.append(pltpu.make_async_copy(source, slab.at[place], sems.at[place]))
        copies[place].start()
    mine = device_in_group()
    owner_copy.wait()

    def block_scan(slot, found):
        begin = visit(slot, mine) * count
        first, second = jnp.int32(-1), jnp.int32(-1)
        for tile in reversed(range(count)):
            hit = owner[begin + tile] == mine
            second = jnp.where(hit, first, second)
            first = jnp.where(hit, begin + tile, first)
        tile = second if wanted else first
        tiles[found] = jnp.maximum(tile, 0)
        slots[found] = slot
        has[slot] = jnp.where(tile >= 0, 1, 0)
        return found + jnp.where(tile >= 0, 1, 0)

    found = lax.fori_loop(0, visits, block_scan, 0)
    for spare in range(2):
        tiles[found + spare] = 0
    index_copy.wait()

    if halves == 1:
        stage, out_sems = refs[-2:]

        def leave(index):
            return pltpu.make_async_copy(stage.at[index], outs[0].at[slots[index]], out_sems.at[index])

        def emit(index, value):
            stage[index] = value

            @pl.when(index < found)
            def _():
                leave(index).start()

    else:
        half = visits // halves

        def emit(index, value):
            for part, out in enumerate(outs):

                @pl.when((index < found) & (slots[index] // half == part))
                def _():
                    out[slots[index] - part * half] = value

    def arrive(place):
        copies[place].wait()
        high, low = split(slab[place])
        parts[0:slab_rows, place * chunk : (place + 1) * chunk] = high
        parts[slab_rows:, place * chunk : (place + 1) * chunk] = low

    def group(step, fresh):
        index = 3 * step
        columns = jnp.concatenate([rows[pl.ds(tiles[index + k], 1), :] for k in range(2)], axis=1)
        total = jnp.zeros((2 * slab_rows, 2 * tile_len), jnp.float32)
        lanes = rows[pl.ds(tiles[index + 2], 1), :]
        lane = jnp.broadcast_to(lanes & (LANES - 1), (SUBLANES, tile_len))
        strip = jnp.broadcast_to(lanes >> 7, (SUBLANES, tile_len))
        picked = [jnp.zeros((SUBLANES, tile_len), jnp.float32)] * (slab_rows // SUBLANES)
        for place in range(CHUNKS):
            begin = place * chunk
            if fresh:
                arrive(place)
            places = lax.broadcasted_iota(jnp.int32, (chunk, 2 * tile_len), 0) + begin
            picks = jnp.where(places == columns, 1.0, 0.0).astype(jnp.bfloat16)
            total += dot(parts[:, begin : begin + chunk], picks)
            for offset in range(0, chunk, LANES):
                inside = strip == (begin + offset) // LANES
                for band in range(slab_rows // SUBLANES):
                    values = slab[place, band * SUBLANES : (band + 1) * SUBLANES, offset : offset + LANES]
                    picked[band] = jnp.where(inside, jnp.take_along_axis(values, lane, axis=1), picked[band])
        total = total[:slab_rows] + total[slab_rows:]
        emit(index, total[:, :tile_len])
        emit(index + 1, total[:, tile_len:])
        emit(index + 2, jnp.concatenate(picked, axis=0))

    @pl.when(found > 0)
    def _():
        group(0, True)

    @pl.when(found == 0)
    def _():
        for copy in copies:
            copy.wait()

    def later(step, carry):
        group(step, False)
        return carry

    lax.fori_loop(1, (found + 2) // 3, later, 0)

    if halves == 1:

        def finish(index, carry):
            leave(index).wait()
            return carry

        lax.fori_loop(0, found, finish, 0)


def gather(wanted, count, visits, halves, visit, parent_slab, rows, owner, after):
    slab_rows, width = parent_slab.shape
    tile_len = rows.shape[1]
    smem = pl.BlockSpec(memory_space=pltpu.SMEM)
    vmem = pl.BlockSpec(memory_space=pltpu.VMEM)
    hbm = pl.BlockSpec(memory_space=pl.ANY)
    scratch = [
        pltpu.VMEM((2 * slab_rows, width), jnp.bfloat16),
        pltpu.VMEM((CHUNKS, slab_rows, width // CHUNKS), jnp.float32),
        pltpu.VMEM(rows.shape, jnp.int32),
        pltpu.SMEM(owner.shape, jnp.int32),
        pltpu.SMEM((visits + 8,), jnp.int32),
        pltpu.SMEM((visits + 8,), jnp.int32),
        pltpu.SemaphoreType.DMA((CHUNKS + 2,)),
    ]
    if halves == 1:
        scratch += [pltpu.VMEM((visits + 2, slab_rows, tile_len), jnp.float32), pltpu.SemaphoreType.DMA((visits + 2,))]
    out = jax.ShapeDtypeStruct((visits // halves, slab_rows, tile_len), jnp.float32)
    return pl.pallas_call(
        functools.partial(gather_kernel, wanted, count, visit, halves),
        out_shape=(out,) * halves + (jax.ShapeDtypeStruct((visits,), jnp.int32),),
        in_specs=[hbm, hbm, hbm, hbm],
        out_specs=(hbm if halves == 1 else vmem,) * halves + (smem,),
        scratch_shapes=scratch,
        compiler_params=pltpu.CompilerParams(vmem_limit_bytes=VMEM_LIMIT),
        cost_estimate=pl.CostEstimate(flops=visits * 4 * slab_rows * width * tile_len, bytes_accessed=8 << 20, transcendentals=0),
    )(after, owner, rows, parent_slab)


def merge_kernel(has, own, passed, *outs):
    for slot, out in enumerate(outs):

        @pl.when(has[slot] > 0)
        def _():
            out[...] = own[slot]

        @pl.when(has[slot] == 0)
        def _():
            out[...] = passed[slot]


def merge(has, own, passed):
    smem = pl.BlockSpec(memory_space=pltpu.SMEM)
    vmem = pl.BlockSpec(memory_space=pltpu.VMEM)
    slots = own.shape[0]
    return pl.pallas_call(
        merge_kernel,
        out_shape=(jax.ShapeDtypeStruct(own.shape[1:], own.dtype),) * slots,
        in_specs=[smem, vmem, vmem],
        out_specs=(vmem,) * slots,
        compiler_params=pltpu.CompilerParams(vmem_limit_bytes=VMEM_LIMIT),
    )(has, own, passed)


def triple(left, right):
    left_high, left_low = split(left)
    right_high, right_low = split(right)
    return dot(
        jnp.concatenate([left_high, left_high, left_low], axis=1),
        jnp.concatenate([right_high, right_low, right_high], axis=0),
    )


def first_kernel(count, owner, me, arrived, panel_in, total, panel, sems):
    steps, depth, _ = panel.shape
    begin = me[0] * count
    copies = [
        pltpu.make_async_copy(panel_in.at[step * depth : (step + 1) * depth, :], panel.at[step], sems.at[step])
        for step in range(steps)
    ]
    for copy in copies:
        copy.start()

    def part(tile):
        return jnp.where(rank_of(owner, tile, begin) == 0, arrived[owner[tile]], 0.0)

    for step in range(steps):
        left = jnp.concatenate([part(begin + 2 * step), part(begin + 2 * step + 1)], axis=1)
        copies[step].wait()
        term = triple(left, panel[step])
        if step == 0:
            total[...] = -term
        else:
            total[...] -= term


def first_product(arrived, panel, owner, me):
    _, slab_rows, tile_len = arrived.shape
    panel_rows, width = panel.shape
    count = panel_rows // tile_len
    smem = pl.BlockSpec(memory_space=pltpu.SMEM)
    vmem = pl.BlockSpec(memory_space=pltpu.VMEM)
    return pl.pallas_call(
        functools.partial(first_kernel, count),
        out_shape=jax.ShapeDtypeStruct((slab_rows, width), jnp.float32),
        in_specs=[smem, smem, vmem, pl.BlockSpec(memory_space=pl.ANY)],
        out_specs=vmem,
        scratch_shapes=[
            pltpu.VMEM((count // 2, 2 * tile_len, width), jnp.float32),
            pltpu.SemaphoreType.DMA((count // 2,)),
        ],
        compiler_params=pltpu.CompilerParams(vmem_limit_bytes=VMEM_LIMIT),
        cost_estimate=pl.CostEstimate(flops=6 * slab_rows * width * panel_rows, bytes_accessed=16 << 20, transcendentals=0),
    )(owner, me, arrived, panel)


def second_kernel(count, place_of, owner, first, *refs):
    *arrived, panel, out, left, held, tiles, sems = refs
    tile_len = held.shape[0] // sems.shape[0]
    mine = device_in_group()
    begin = mine * count
    width = out.shape[2]

    def copy(tile, slot):
        source = panel.at[pl.ds(pl.multiple_of((tile - begin) * tile_len, tile_len), tile_len), :]
        target = held.at[pl.ds(pl.multiple_of(slot * tile_len, tile_len), tile_len), :]
        return pltpu.make_async_copy(source, target, sems.at[slot])

    names = [owner[begin + tile] for tile in range(count)]
    found = jnp.int32(0)
    for tile in range(1, count):
        hit = functools.reduce(jnp.logical_or, [names[tile] == name for name in names[:tile]])

        @pl.when(hit)
        def _():
            tiles[found] = begin + tile
            copy(begin + tile, found).start()

        found = found + jnp.where(hit, 1, 0)

    @pl.when(lax.rem(found, 2) == 1)
    def _():
        left[:, tile_len:] = jnp.zeros_like(left[:, tile_len:])
        held[pl.ds(pl.multiple_of(found * tile_len, tile_len), tile_len), :] = jnp.zeros((tile_len, held.shape[1]), jnp.float32)

    def side(slot, begin_lane):
        tile = tiles[slot]
        place = place_of(owner[tile], mine)
        for index, ref in enumerate(arrived):

            @pl.when(place == index)
            def _():
                left[:, begin_lane : begin_lane + tile_len] = ref[...]

        copy(tile, slot).wait()

    def pair(step):
        side(2 * step, 0)

        @pl.when(2 * step + 1 < found)
        def _():
            side(2 * step + 1, tile_len)

        rows = pl.ds(pl.multiple_of(2 * step * tile_len, 2 * tile_len), 2 * tile_len)
        return triple(left[...], held[rows, :])

    @pl.when(found > 0)
    def _():
        term = pair(0)
        for block in range(out.shape[0]):
            columns = slice(block * width, (block + 1) * width)
            out[block] = first[:, columns] - term[:, columns]

    @pl.when(found == 0)
    def _():
        for block in range(out.shape[0]):
            out[block] = first[:, block * width : (block + 1) * width]

    def later(step, carry):
        @pl.when(2 * step + 1 >= found)
        def _():
            left[:, tile_len:] = jnp.zeros_like(left[:, tile_len:])

        term = pair(step)
        for block in range(out.shape[0]):
            out[block] -= term[:, block * width : (block + 1) * width]
        return carry

    lax.fori_loop(1, (found + 1) // 2, later, 0)


def second_product(first, arrived, place_of, panel, owner, me, blocks):
    slab_rows, tile_len = arrived[0].shape
    panel_rows, width = panel.shape
    count = panel_rows // tile_len
    most = count // CAP
    smem = pl.BlockSpec(memory_space=pltpu.SMEM)
    vmem = pl.BlockSpec(memory_space=pltpu.VMEM)
    return pl.pallas_call(
        functools.partial(second_kernel, count, place_of),
        out_shape=jax.ShapeDtypeStruct((blocks, slab_rows, width // blocks), jnp.float32),
        in_specs=[smem, vmem] + [vmem] * len(arrived) + [pl.BlockSpec(memory_space=pl.ANY)],
        out_specs=vmem,
        scratch_shapes=[
            pltpu.VMEM((slab_rows, 2 * tile_len), jnp.float32),
            pltpu.VMEM((most * tile_len, width), jnp.float32),
            pltpu.SMEM((most + 8,), jnp.int32),
            pltpu.SemaphoreType.DMA((most,)),
        ],
        compiler_params=pltpu.CompilerParams(vmem_limit_bytes=VMEM_LIMIT),
    )(owner, first, *arrived, panel)


def diag_kernel(terms, slab_panel, inverse, out):
    total = jnp.sum(terms[...], axis=0)
    inverse[...] = total
    right_high, right_low = split(total)
    left_high, left_low = split(slab_panel[...])
    both = ((0,), (0,))
    result = dot(left_high, right_high, both) + dot(left_high, right_low, both) + dot(left_low, right_high, both)
    out[...] = result.reshape(out.shape)


def diag_terms(terms, slab_panel, blocks):
    _, slab_rows, width = terms.shape
    rows = slab_panel.shape[1]
    vmem = pl.BlockSpec(memory_space=pltpu.VMEM)
    return pl.pallas_call(
        diag_kernel,
        out_shape=(
            jax.ShapeDtypeStruct((slab_rows, width), jnp.float32),
            jax.ShapeDtypeStruct((blocks, rows // blocks, width), jnp.float32),
        ),
        in_specs=[vmem, vmem],
        out_specs=(vmem, vmem),
        compiler_params=pltpu.CompilerParams(vmem_limit_bytes=VMEM_LIMIT),
    )(terms, slab_panel)


def local(parent_slab, panel, slab_panel, diag_inverse, tile_rows, tile_owner):
    row_count, col_count = lax.axis_size("row"), lax.axis_size("col")
    group_size = lax.axis_size("child") * row_count
    me = (lax.axis_index("child") * row_count + lax.axis_index("row")).astype(jnp.int32).reshape(1)
    owner = tile_owner.reshape(-1)
    rows = tile_rows.reshape(-1, tile_rows.shape[2])
    count = owner.shape[0] // group_size

    def by_child(slot, mine):
        row = lax.rem(mine, row_count)
        child = mine // row_count + slot // row_count
        return lax.rem(child * row_count + lax.rem(row + slot, row_count), group_size)

    first_columns, _ = gather(0, count, group_size, 1, lambda slot, mine: slot, parent_slab, rows, owner, me)
    after = lax.optimization_barrier((me, first_columns))[0]
    first_arrived = lax.all_to_all(first_columns, ("child", "row"), split_axis=0, concat_axis=0, tiled=True)
    own, other, has = gather(1, count, group_size, 2, by_child, parent_slab, rows, owner, after)
    passed = lax.ppermute(other, "child", [(0, 1), (1, 0)])
    merged = merge(has, own, passed)
    second_arrived = [merged[0]] + [None] * (row_count - 1)
    for step in sorted(range(1, row_count), key=lambda step: min(step, row_count - step)):
        route = [(row, (row + step) % row_count) for row in range(row_count)]
        second_arrived[step] = lax.ppermute(merged[step], "row", route)
    first = first_product(first_arrived, panel[0], owner, lax.optimization_barrier((me, *merged))[0])
    blocks = lax.optimization_barrier((owner, first_columns))[0].reshape(group_size, count)
    twice = jnp.sum((blocks[:, :, None] == jnp.arange(group_size)).astype(jnp.int32), axis=1) > 1
    single = ~jnp.any(twice[:, :row_count] & twice[:, row_count:])

    def merged_sends(first, *arrived):
        def place_of(own, mine):
            return lax.rem(mine - own + group_size, row_count)

        return second_product(first, arrived, place_of, panel[0], owner, me, row_count)

    def all_sends(first, *arrived):
        columns, _ = gather(1, count, group_size, 1, lambda slot, mine: slot, parent_slab, rows, owner, me)
        columns = lax.all_to_all(columns, ("child", "row"), split_axis=0, concat_axis=0, tiled=True)
        arrived = [columns[place] for place in range(group_size)]
        return second_product(first, arrived, lambda own, mine: own, panel[0], owner, me, row_count)

    partial = lax.cond(single, merged_sends, all_sends, first, *second_arrived)
    terms = lax.all_to_all(partial, "row", split_axis=0, concat_axis=0, tiled=True)
    slab_inverse, parts = diag_terms(terms, slab_panel[0], col_count)
    reduced = lax.all_to_all(parts, "col", split_axis=0, concat_axis=0, tiled=True)
    diag_block = diag_inverse[0] - jnp.sum(reduced, axis=0)
    return slab_inverse[None], diag_block[None]


def solution(mesh):
    in_specs = (
        P("col", ("child", "row")),
        P("child", "row", None),
        P("child", "col", None),
        P("child", "col", "row"),
        P(),
        P(),
    )
    out_specs = (P("child", "col", "row"), P("child", "col", "row"))
    return jax.shard_map(local, mesh=mesh, in_specs=in_specs, out_specs=out_specs, check_vma=False)
```

```python
import functools

import jax
import jax.numpy as jnp
from jax import lax
from jax.experimental import pallas as pl
from jax.experimental.pallas import tpu as pltpu
from jax.sharding import PartitionSpec as P

CAP = 2
VMEM_LIMIT = 48 << 20
CHUNKS = 5
LANES = 128
SUBLANES = 8


def split(value):
    high = value.astype(jnp.bfloat16)
    low = (value - high.astype(jnp.float32)).astype(jnp.bfloat16)
    return high, low


def dot(left, right, contract=((1,), (0,))):
    return lax.dot_general(left, right, (contract, ((), ())), preferred_element_type=jnp.float32)


def rank_of(owner, tile, first):
    own = owner[tile]

    def earlier(other, rank):
        return rank + jnp.where(owner[other] == own, 1, 0)

    return lax.fori_loop(first, tile, earlier, 0)


def device_in_group():
    return lax.axis_index("child") * lax.axis_size("row") + lax.axis_index("row")


def gather_kernel(wanted, count, visit, halves, after, owner_in, rows_in, slab_in, *refs):
    outs, has, (parts, slab, rows, owner, tiles, slots, sems) = refs[:halves], refs[halves], refs[halves + 1 :][:7]
    _, slab_rows, chunk = slab.shape
    tile_len = rows.shape[1]
    visits = has.shape[0]
    owner_copy = pltpu.make_async_copy(owner_in, owner, sems.at[CHUNKS + 1])
    owner_copy.start()
    index_copy = pltpu.make_async_copy(rows_in, rows, sems.at[CHUNKS])
    index_copy.start()
    copies = []
    for place in range(CHUNKS):
        source = slab_in.at[:, place * chunk : (place + 1) * chunk]
        copies.append(pltpu.make_async_copy(source, slab.at[place], sems.at[place]))
        copies[place].start()
    mine = device_in_group()
    owner_copy.wait()

    def block_scan(slot, found):
        begin = visit(slot, mine) * count
        first, second = jnp.int32(-1), jnp.int32(-1)
        for tile in reversed(range(count)):
            hit = owner[begin + tile] == mine
            second = jnp.where(hit, first, second)
            first = jnp.where(hit, begin + tile, first)
        tile = second if wanted else first
        tiles[found] = jnp.maximum(tile, 0)
        slots[found] = slot
        has[slot] = jnp.where(tile >= 0, 1, 0)
        return found + jnp.where(tile >= 0, 1, 0)

    found = lax.fori_loop(0, visits, block_scan, 0)
    for spare in range(2):
        tiles[found + spare] = 0
    index_copy.wait()

    if halves == 1:
        stage, out_sems = refs[-2:]

        def leave(index):
            return pltpu.make_async_copy(stage.at[index], outs[0].at[slots[index]], out_sems.at[index])

        def emit(index, value):
            stage[index] = value

            @pl.when(index < found)
            def _():
                leave(index).start()

    else:
        half = visits // halves

        def emit(index, value):
            for part, out in enumerate(outs):

                @pl.when((index < found) & (slots[index] // half == part))
                def _():
                    out[slots[index] - part * half] = value

    def arrive(place):
        copies[place].wait()
        high, low = split(slab[place])
        parts[0:slab_rows, place * chunk : (place + 1) * chunk] = high
        parts[slab_rows:, place * chunk : (place + 1) * chunk] = low

    def group(step, fresh):
        index = 3 * step
        columns = jnp.concatenate([rows[pl.ds(tiles[index + k], 1), :] for k in range(2)], axis=1)
        total = jnp.zeros((2 * slab_rows, 2 * tile_len), jnp.float32)
        lanes = rows[pl.ds(tiles[index + 2], 1), :]
        lane = jnp.broadcast_to(lanes & (LANES - 1), (SUBLANES, tile_len))
        strip = jnp.broadcast_to(lanes >> 7, (SUBLANES, tile_len))
        picked = [jnp.zeros((SUBLANES, tile_len), jnp.float32)] * (slab_rows // SUBLANES)
        for place in range(CHUNKS):
            begin = place * chunk
            if fresh:
                arrive(place)
            places = lax.broadcasted_iota(jnp.int32, (chunk, 2 * tile_len), 0) + begin
            picks = jnp.where(places == columns, 1.0, 0.0).astype(jnp.bfloat16)
            total += dot(parts[:, begin : begin + chunk], picks)
            for offset in range(0, chunk, LANES):
                inside = strip == (begin + offset) // LANES
                for band in range(slab_rows // SUBLANES):
                    values = slab[place, band * SUBLANES : (band + 1) * SUBLANES, offset : offset + LANES]
                    picked[band] = jnp.where(inside, jnp.take_along_axis(values, lane, axis=1), picked[band])
        total = total[:slab_rows] + total[slab_rows:]
        emit(index, total[:, :tile_len])
        emit(index + 1, total[:, tile_len:])
        emit(index + 2, jnp.concatenate(picked, axis=0))

    @pl.when(found > 0)
    def _():
        group(0, True)

    @pl.when(found == 0)
    def _():
        for copy in copies:
            copy.wait()

    def later(step, carry):
        group(step, False)
        return carry

    lax.fori_loop(1, (found + 2) // 3, later, 0)

    if halves == 1:

        def finish(index, carry):
            leave(index).wait()
            return carry

        lax.fori_loop(0, found, finish, 0)


def gather(wanted, count, visits, halves, visit, parent_slab, rows, owner, after):
    slab_rows, width = parent_slab.shape
    tile_len = rows.shape[1]
    smem = pl.BlockSpec(memory_space=pltpu.SMEM)
    vmem = pl.BlockSpec(memory_space=pltpu.VMEM)
    hbm = pl.BlockSpec(memory_space=pl.ANY)
    scratch = [
        pltpu.VMEM((2 * slab_rows, width), jnp.bfloat16),
        pltpu.VMEM((CHUNKS, slab_rows, width // CHUNKS), jnp.float32),
        pltpu.VMEM(rows.shape, jnp.int32),
        pltpu.SMEM(owner.shape, jnp.int32),
        pltpu.SMEM((visits + 8,), jnp.int32),
        pltpu.SMEM((visits + 8,), jnp.int32),
        pltpu.SemaphoreType.DMA((CHUNKS + 2,)),
    ]
    if halves == 1:
        scratch += [pltpu.VMEM((visits + 2, slab_rows, tile_len), jnp.float32), pltpu.SemaphoreType.DMA((visits + 2,))]
    out = jax.ShapeDtypeStruct((visits // halves, slab_rows, tile_len), jnp.float32)
    return pl.pallas_call(
        functools.partial(gather_kernel, wanted, count, visit, halves),
        out_shape=(out,) * halves + (jax.ShapeDtypeStruct((visits,), jnp.int32),),
        in_specs=[hbm, hbm, hbm, hbm],
        out_specs=(hbm if halves == 1 else vmem,) * halves + (smem,),
        scratch_shapes=scratch,
        compiler_params=pltpu.CompilerParams(vmem_limit_bytes=VMEM_LIMIT),
        cost_estimate=pl.CostEstimate(flops=visits * 4 * slab_rows * width * tile_len, bytes_accessed=8 << 20, transcendentals=0),
    )(after, owner, rows, parent_slab)


def merge_kernel(has, own, passed, *outs):
    for slot, out in enumerate(outs):

        @pl.when(has[slot] > 0)
        def _():
            out[...] = own[slot]

        @pl.when(has[slot] == 0)
        def _():
            out[...] = passed[slot]


def merge(has, own, passed):
    smem = pl.BlockSpec(memory_space=pltpu.SMEM)
    vmem = pl.BlockSpec(memory_space=pltpu.VMEM)
    slots = own.shape[0]
    return pl.pallas_call(
        merge_kernel,
        out_shape=(jax.ShapeDtypeStruct(own.shape[1:], own.dtype),) * slots,
        in_specs=[smem, vmem, vmem],
        out_specs=(vmem,) * slots,
        compiler_params=pltpu.CompilerParams(vmem_limit_bytes=VMEM_LIMIT),
    )(has, own, passed)


def triple(left, right):
    left_high, left_low = split(left)
    right_high, right_low = split(right)
    return dot(
        jnp.concatenate([left_high, left_high, left_low], axis=1),
        jnp.concatenate([right_high, right_low, right_high], axis=0),
    )


def first_kernel(count, owner, me, arrived, panel_in, total, panel, sems):
    steps, depth, _ = panel.shape
    begin = me[0] * count
    copies = [
        pltpu.make_async_copy(panel_in.at[step * depth : (step + 1) * depth, :], panel.at[step], sems.at[step])
        for step in range(steps)
    ]
    for copy in copies:
        copy.start()

    def part(tile):
        return jnp.where(rank_of(owner, tile, begin) == 0, arrived[owner[tile]], 0.0)

    for step in range(steps):
        left = jnp.concatenate([part(begin + 2 * step), part(begin + 2 * step + 1)], axis=1)
        copies[step].wait()
        term = triple(left, panel[step])
        if step == 0:
            total[...] = -term
        else:
            total[...] -= term


def first_product(arrived, panel, owner, me):
    _, slab_rows, tile_len = arrived.shape
    panel_rows, width = panel.shape
    count = panel_rows // tile_len
    smem = pl.BlockSpec(memory_space=pltpu.SMEM)
    vmem = pl.BlockSpec(memory_space=pltpu.VMEM)
    return pl.pallas_call(
        functools.partial(first_kernel, count),
        out_shape=jax.ShapeDtypeStruct((slab_rows, width), jnp.float32),
        in_specs=[smem, smem, vmem, pl.BlockSpec(memory_space=pl.ANY)],
        out_specs=vmem,
        scratch_shapes=[
            pltpu.VMEM((count // 2, 2 * tile_len, width), jnp.float32),
            pltpu.SemaphoreType.DMA((count // 2,)),
        ],
        compiler_params=pltpu.CompilerParams(vmem_limit_bytes=VMEM_LIMIT),
        cost_estimate=pl.CostEstimate(flops=6 * slab_rows * width * panel_rows, bytes_accessed=16 << 20, transcendentals=0),
    )(owner, me, arrived, panel)


def second_kernel(count, place_of, owner, first, *refs):
    *arrived, panel, out, left, held, tiles, sems = refs
    tile_len = held.shape[0] // sems.shape[0]
    mine = device_in_group()
    begin = mine * count
    width = out.shape[2]
    blocks = out.shape[0]

    def ahead(block):
        return lax.rem(block + blocks - lax.rem(mine, blocks), blocks)

    def copy(tile, slot):
        source = panel.at[pl.ds(pl.multiple_of((tile - begin) * tile_len, tile_len), tile_len), :]
        target = held.at[pl.ds(pl.multiple_of(slot * tile_len, tile_len), tile_len), :]
        return pltpu.make_async_copy(source, target, sems.at[slot])

    names = [owner[begin + tile] for tile in range(count)]
    found = jnp.int32(0)
    for tile in range(1, count):
        hit = functools.reduce(jnp.logical_or, [names[tile] == name for name in names[:tile]])

        @pl.when(hit)
        def _():
            tiles[found] = begin + tile
            copy(begin + tile, found).start()

        found = found + jnp.where(hit, 1, 0)

    @pl.when(lax.rem(found, 2) == 1)
    def _():
        left[:, tile_len:] = jnp.zeros_like(left[:, tile_len:])
        held[pl.ds(pl.multiple_of(found * tile_len, tile_len), tile_len), :] = jnp.zeros((tile_len, held.shape[1]), jnp.float32)

    def side(slot, begin_lane):
        tile = tiles[slot]
        place = place_of(owner[tile], mine)
        for index, ref in enumerate(arrived):

            @pl.when(place == index)
            def _():
                left[:, begin_lane : begin_lane + tile_len] = ref[...]

        copy(tile, slot).wait()

    def pair(step):
        side(2 * step, 0)

        @pl.when(2 * step + 1 < found)
        def _():
            side(2 * step + 1, tile_len)

        rows = pl.ds(pl.multiple_of(2 * step * tile_len, 2 * tile_len), 2 * tile_len)
        return triple(left[...], held[rows, :])

    @pl.when(found > 0)
    def _():
        term = pair(0)
        for block in range(out.shape[0]):
            columns = slice(block * width, (block + 1) * width)
            out[ahead(block)] = first[:, columns] - term[:, columns]

    @pl.when(found == 0)
    def _():
        for block in range(out.shape[0]):
            out[ahead(block)] = first[:, block * width : (block + 1) * width]

    def later(step, carry):
        @pl.when(2 * step + 1 >= found)
        def _():
            left[:, tile_len:] = jnp.zeros_like(left[:, tile_len:])

        term = pair(step)
        for block in range(out.shape[0]):
            out[ahead(block)] -= term[:, block * width : (block + 1) * width]
        return carry

    lax.fori_loop(1, (found + 1) // 2, later, 0)


def second_product(first, arrived, place_of, panel, owner, me, blocks):
    slab_rows, tile_len = arrived[0].shape
    panel_rows, width = panel.shape
    count = panel_rows // tile_len
    most = count // CAP
    smem = pl.BlockSpec(memory_space=pltpu.SMEM)
    vmem = pl.BlockSpec(memory_space=pltpu.VMEM)
    return pl.pallas_call(
        functools.partial(second_kernel, count, place_of),
        out_shape=jax.ShapeDtypeStruct((blocks, slab_rows, width // blocks), jnp.float32),
        in_specs=[smem, vmem] + [vmem] * len(arrived) + [pl.BlockSpec(memory_space=pl.ANY)],
        out_specs=vmem,
        scratch_shapes=[
            pltpu.VMEM((slab_rows, 2 * tile_len), jnp.float32),
            pltpu.VMEM((most * tile_len, width), jnp.float32),
            pltpu.SMEM((most + 8,), jnp.int32),
            pltpu.SemaphoreType.DMA((most,)),
        ],
        compiler_params=pltpu.CompilerParams(vmem_limit_bytes=VMEM_LIMIT),
    )(owner, first, *arrived, panel)


def diag_kernel(*refs):
    *terms, slab_panel, inverse, out = refs
    total = sum(term[...] for term in terms[1:]) + terms[0][...]
    inverse[...] = total
    right_high, right_low = split(total)
    left_high, left_low = split(slab_panel[...])
    both = ((0,), (0,))
    result = dot(left_high, right_high, both) + dot(left_high, right_low, both) + dot(left_low, right_high, both)
    out[...] = result.reshape(out.shape)


def diag_terms(terms, slab_panel, blocks):
    slab_rows, width = terms[0].shape
    rows = slab_panel.shape[1]
    vmem = pl.BlockSpec(memory_space=pltpu.VMEM)
    return pl.pallas_call(
        diag_kernel,
        out_shape=(
            jax.ShapeDtypeStruct((slab_rows, width), jnp.float32),
            jax.ShapeDtypeStruct((blocks, rows // blocks, width), jnp.float32),
        ),
        in_specs=[vmem] * (len(terms) + 1),
        out_specs=(vmem, vmem),
        compiler_params=pltpu.CompilerParams(vmem_limit_bytes=VMEM_LIMIT),
    )(*terms, slab_panel)


def local(parent_slab, panel, slab_panel, diag_inverse, tile_rows, tile_owner):
    row_count, col_count = lax.axis_size("row"), lax.axis_size("col")
    group_size = lax.axis_size("child") * row_count
    me = (lax.axis_index("child") * row_count + lax.axis_index("row")).astype(jnp.int32).reshape(1)
    owner = tile_owner.reshape(-1)
    rows = tile_rows.reshape(-1, tile_rows.shape[2])
    count = owner.shape[0] // group_size

    def by_child(slot, mine):
        row = lax.rem(mine, row_count)
        child = mine // row_count + slot // row_count
        return lax.rem(child * row_count + lax.rem(row + slot, row_count), group_size)

    first_columns, _ = gather(0, count, group_size, 1, lambda slot, mine: slot, parent_slab, rows, owner, me)
    after = lax.optimization_barrier((me, first_columns))[0]
    first_arrived = lax.all_to_all(first_columns, ("child", "row"), split_axis=0, concat_axis=0, tiled=True)
    own, other, has = gather(1, count, group_size, 2, by_child, parent_slab, rows, owner, after)
    passed = lax.ppermute(other, "child", [(0, 1), (1, 0)])
    merged = merge(has, own, passed)
    second_arrived = [merged[0]] + [None] * (row_count - 1)
    for step in sorted(range(1, row_count), key=lambda step: min(step, row_count - step)):
        route = [(row, (row + step) % row_count) for row in range(row_count)]
        second_arrived[step] = lax.ppermute(merged[step], "row", route)
    first = first_product(first_arrived, panel[0], owner, lax.optimization_barrier((me, *merged))[0])
    blocks = lax.optimization_barrier((owner, first_columns))[0].reshape(group_size, count)
    twice = jnp.sum((blocks[:, :, None] == jnp.arange(group_size)).astype(jnp.int32), axis=1) > 1
    single = ~jnp.any(twice[:, :row_count] & twice[:, row_count:])

    def merged_sends(first, *arrived):
        def place_of(own, mine):
            return lax.rem(mine - own + group_size, row_count)

        return second_product(first, arrived, place_of, panel[0], owner, me, row_count)

    def all_sends(first, *arrived):
        columns, _ = gather(1, count, group_size, 1, lambda slot, mine: slot, parent_slab, rows, owner, me)
        columns = lax.all_to_all(columns, ("child", "row"), split_axis=0, concat_axis=0, tiled=True)
        arrived = [columns[place] for place in range(group_size)]
        return second_product(first, arrived, lambda own, mine: own, panel[0], owner, me, row_count)

    partial = lax.cond(single, merged_sends, all_sends, first, *second_arrived)
    terms = [partial[0]]
    for step in range(1, row_count):
        route = [(row, (row + step) % row_count) for row in range(row_count)]
        terms.append(lax.ppermute(partial[step], "row", route))
    slab_inverse, parts = diag_terms(terms, slab_panel[0], col_count)
    reduced = lax.all_to_all(parts, "col", split_axis=0, concat_axis=0, tiled=True)
    diag_block = diag_inverse[0] - jnp.sum(reduced, axis=0)
    return slab_inverse[None], diag_block[None]


def solution(mesh):
    in_specs = (
        P("col", ("child", "row")),
        P("child", "row", None),
        P("child", "col", None),
        P("child", "col", "row"),
        P(),
        P(),
    )
    out_specs = (P("child", "col", "row"), P("child", "col", "row"))
    return jax.shard_map(local, mesh=mesh, in_specs=in_specs, out_specs=out_specs, check_vma=False)
```
